128 devices in a mesh: ta: 16 (over x_hi, y, core), ha: 8 (over x_lo, z).
Axes of the slice: x: 4 (x_hi: 2, x_lo: 2; x = x_hi * 2 + x_lo), y: 4, z: 4, core: 2. Of those that a mesh axis runs over, the one named last changes fastest.
Arguments:
- activations: bfloat16 [32, 32, 80, 1536], P('ta', 'ha'), may hold values from -6 to 6
- qkv_weight: bfloat16 [1536, 4608], replicated, may hold values from -0.15625 to 0.15625
- out_weight: bfloat16 [1536, 1536], replicated, may hold values from -0.15625 to 0.15625
- query_gain: float32 [128], replicated, may hold values from 0.8 to 2.5
- key_gain: float32 [128], replicated, may hold values from 0.8 to 2.5
- clip_lengths: int32 [4], replicated, may hold values from 1 to 16, 32 in all
- extents: int32 [16, 8, 2], replicated, may hold values from 0 to 1
Outputs:
- mixed: bfloat16 [32, 32, 80, 1536], P('ta', 'ha')
The draws below stay inside these ranges and needn't reach their ends.
Inputs may be any that keep to these rules, and one draw needn't show every extreme that they name: `extents`: each is a reach of 0 or 1 tiles. `clip_lengths`: the 4 lengths sum to 32.
All inputs are finite; a program needn't handle non-finite values.
Results may differ from the reference program's by a relative error of at most 0.011.
Values may be sent and summed in bfloat16 or wider, within the bound.
No kernel may reach another device: no remote copies, remote signals or barrier semaphores. Data moves between devices by JAX's collectives and lax.ppermute only.
A program may use at most 256 MiB of HBM per device.

```python
import math
import jax
import jax.numpy as jnp
import numpy as np
from jax import lax

D = 1536
HEADS = 12
HD = 128
COLS = 80
FT = 2
RH = 4
NCLIP = 4
TTILES = 16
HTILES = 8
FRAMES = 32
ROWS = 32


def place_ends(drawn, own_key, low, top_value):
    longest = drawn.shape.index(max(drawn.shape))
    spots = []
    for shift in (0, 1):
        where = [jax.random.randint(jax.random.fold_in(own_key, axis), (), 0, length) for axis, length in enumerate(drawn.shape)]
        where[longest] = (where[longest] + shift) % drawn.shape[longest]
        spots.append(tuple(where))
    return drawn.at[spots[0]].set(low).at[spots[1]].set(top_value)


def block_scale(stream_key, dims, shards, smallest, top_value):
    loudness = 1.0
    for dim, shards_of in shards:
        draws = jax.random.uniform(jax.random.fold_in(jax.random.fold_in(stream_key, 6), dim), (shards_of,), jnp.float32, smallest / len(shards), top_value / len(shards))
        loudness = loudness * jnp.repeat(jnp.exp(draws), dims[dim] // shards_of).reshape((-1,) + (1,) * (len(dims) - 1 - dim))
    return loudness


def length_profile(count, total, limit, skew):
    weights = [(1 << 20) // math.isqrt(standing ** skew) + 1 for standing in range(2, count + 1)]
    spare, counts = total - limit - (count - 1), [1] * (count - 1)
    while spare > 0:
        movable = [i for i in range(count - 1) if counts[i] < limit]
        pool, left = sum([weights[i] for i in movable]), spare
        for i in movable:
            more = min(limit - counts[i], max(1, left * weights[i] // pool), spare)
            counts[i] = counts[i] + more
            spare = spare - more
    return np.array([limit] + counts)


def ragged_sizes(rng, number_of, total, limit, lean):
    if number_of == 2:
        one = jax.random.randint(rng, (), max(1, total - limit), min(limit, total - 1) + 1)
        return jnp.stack([one, total - one])
    lengths = jnp.asarray(length_profile(number_of, total, limit, lean), jnp.int32)
    couples = (number_of - 1) // 2
    source_of, taker = lengths[1:1 + 2 * couples:2], lengths[2:2 + 2 * couples:2]
    slack = jnp.minimum(source_of - 1, limit - taker)
    shifted = jax.random.randint(jax.random.fold_in(rng, 1), (couples,), 0, 1 << 20) % (slack + 1)
    lengths = lengths.at[1:1 + 2 * couples:2].set(source_of - shifted).at[2:2 + 2 * couples:2].set(taker + shifted)
    return lengths[jax.random.permutation(jax.random.fold_in(rng, 2), number_of)]


def noise(rng, extent, scale, bound, shards=(), kind=jnp.bfloat16):
    entries = scale * jax.random.normal(rng, extent, jnp.float32)
    if shards:
        entries = entries * block_scale(rng, extent, shards, -0.22, 0.18)
    return jnp.clip(entries, -bound, bound).astype(kind)


def setup_inputs(seed: int = 0) -> dict:
    splits = jax.random.split(jax.random.key(seed), 8)
    activations = noise(splits[0], (FRAMES, ROWS, COLS, D), 1.0, 6.0, ((0, 16), (1, 8)))
    qkv_weight = noise(splits[1], (D, 3 * HEADS * HD), D ** -0.5, 0.15625)
    out_weight = noise(splits[2], (HEADS * HD, D), (HEADS * HD) ** -0.5, 0.15625)
    query_gain = jnp.clip(jnp.exp(jax.random.uniform(splits[3], (HD,), jnp.float32, math.log(0.8), math.log(2.5))), 0.8, 2.5)
    key_gain = jnp.clip(jnp.exp(jax.random.uniform(splits[4], (HD,), jnp.float32, math.log(0.8), math.log(2.5))), 0.8, 2.5)
    clip_lengths = ragged_sizes(splits[5], NCLIP, FRAMES, FRAMES // 2, 1).astype(jnp.int32)
    extents = place_ends(jax.random.randint(splits[6], (TTILES, HTILES, 2), 0, 2), jax.random.fold_in(splits[6], 1), 0, 1).astype(jnp.int32)
    return dict(activations=activations, qkv_weight=qkv_weight, out_weight=out_weight, query_gain=query_gain, key_gain=key_gain, clip_lengths=clip_lengths, extents=extents)


norm_eps = 1e-06

def normalize(features, gain_vec):
    mean_sq = lax.optimization_barrier(jnp.mean(features * features, axis=-1, keepdims=True))
    return features * lax.rsqrt(mean_sq + norm_eps) * gain_vec

def frame_clips(frame_index, clip_ends):
    return lax.optimization_barrier(jnp.sum((frame_index[..., None] >= clip_ends).astype(jnp.int32), axis=-1))

def to_tiles(layout_in, ttiles, htiles):
    trailing = layout_in.shape[3:]
    shaped = layout_in.reshape((ttiles, FT, htiles, RH, COLS) + trailing)
    axes_order = (0, 2, 1, 3, 4) + tuple(range(5, 5 + len(trailing)))
    return shaped.transpose(axes_order).reshape((ttiles, htiles, FT * RH * COLS) + trailing)

def reference(activations, qkv_weight, out_weight, query_gain, key_gain, clip_lengths, extents):
    inner_width = HEADS * HD
    ttiles = FRAMES // FT
    htiles = ROWS // RH
    tile_len = FT * RH * COLS
    flattened = activations.reshape(-1, D)
    projected = jnp.dot(flattened, qkv_weight, preferred_element_type=jnp.float32)
    head_shape = (FRAMES, ROWS, COLS, HEADS, HD)
    queries = normalize(projected[:, :inner_width].reshape(head_shape), query_gain).astype(jnp.bfloat16)
    key_rows = normalize(projected[:, inner_width:2 * inner_width].reshape(head_shape), key_gain).astype(jnp.bfloat16)
    value_rows = projected[:, 2 * inner_width:].reshape(head_shape).astype(jnp.bfloat16)
    query_tiles = to_tiles(queries, ttiles, htiles)
    key_pad = jnp.pad(to_tiles(key_rows, ttiles, htiles), ((1, 1), (1, 1), (0, 0), (0, 0), (0, 0)))
    value_pad = jnp.pad(to_tiles(value_rows, ttiles, htiles), ((1, 1), (1, 1), (0, 0), (0, 0), (0, 0)))
    clip_ends = jnp.cumsum(clip_lengths).astype(jnp.int32)
    frame_clip = frame_clips(jnp.arange(FRAMES, dtype=jnp.int32), clip_ends)
    tile_clip = jnp.repeat(frame_clip.reshape(ttiles, FT), RH * COLS, axis=1)
    clip_pad = jnp.pad(tile_clip, ((1, 1), (0, 0)), constant_values=-1)
    score_scale = HD ** (-0.5)
    zero_idx = jnp.zeros((), jnp.int32)

    def one_tile(position):
        time_pos = (position // htiles).astype(jnp.int32)
        height_pos = (position % htiles).astype(jnp.int32)
        query_rows = query_tiles[time_pos, height_pos].astype(jnp.float32)
        starts = (time_pos, height_pos, zero_idx, zero_idx, zero_idx)
        near_keys = lax.dynamic_slice(key_pad, starts, (3, 3, tile_len, HEADS, HD)).reshape(9 * tile_len, HEADS, HD).astype(jnp.float32)
        near_vals = lax.dynamic_slice(value_pad, starts, (3, 3, tile_len, HEADS, HD)).reshape(9 * tile_len, HEADS, HD).astype(jnp.float32)
        near_clip = lax.dynamic_slice(clip_pad, (time_pos, zero_idx), (3, tile_len))
        reach_pair = extents[time_pos, height_pos]
        step_t = jnp.arange(3, dtype=jnp.int32) - 1
        step_h = jnp.arange(3, dtype=jnp.int32) - 1
        time_ok = (jnp.abs(step_t) <= reach_pair[0]) & (time_pos + step_t >= 0) & (time_pos + step_t < ttiles)
        height_ok = (jnp.abs(step_h) <= reach_pair[1]) & (height_pos + step_h >= 0) & (height_pos + step_h < htiles)
        slot_ok = time_ok[:, None] & height_ok[None, :]
        key_ok = jnp.broadcast_to(slot_ok[:, :, None], (3, 3, tile_len)).reshape(9 * tile_len)
        key_clip = jnp.broadcast_to(near_clip[:, None, :], (3, 3, tile_len)).reshape(9 * tile_len)
        query_clip = tile_clip[time_pos]
        allowed = key_ok[None, :] & (query_clip[:, None] == key_clip[None, :])
        scores = jnp.einsum('qhd,khd->hqk', query_rows, near_keys) * score_scale
        weights = jnp.where(allowed[None], jnp.exp(scores), 0.0)
        total = lax.optimization_barrier(jnp.sum(weights, axis=-1))
        rounded = lax.optimization_barrier(weights.astype(jnp.bfloat16)).astype(jnp.float32)
        summed = jnp.einsum('hqk,khd->qhd', rounded, near_vals)
        attended = summed / total.T[:, :, None]
        return attended.reshape(tile_len, inner_width).astype(jnp.bfloat16)
    attended = lax.map(one_tile, jnp.arange(ttiles * htiles, dtype=jnp.int32))
    result = jnp.dot(attended.reshape(-1, inner_width), out_weight, preferred_element_type=jnp.float32).astype(jnp.bfloat16)
    result = result.reshape(ttiles, htiles, FT, RH, COLS, D).transpose(0, 2, 1, 3, 4, 5)
    return result.reshape(FRAMES, ROWS, COLS, D)
```

```python
import functools
import math

import jax
import jax.numpy as jnp
from jax import lax
from jax.experimental import pallas as pl
from jax.experimental.pallas import tpu as pltpu
from jax.sharding import PartitionSpec as P

norm_eps = 1e-06
f32 = jnp.float32
bf16 = jnp.bfloat16
hd = 128
group = 4
kinds = ("own", "core", "y")
vmem_bytes = 44 << 20


def normed(features, gain):
    mean_sq = jnp.mean(features * features, axis=-1, keepdims=True)
    return (features * lax.rsqrt(mean_sq + norm_eps) * gain).astype(bf16)


def same_clip(first, second, lengths):
    end = 0
    same = None
    for c in range(lengths.shape[0] - 1):
        end = end + lengths[c]
        here = (first >= end) == (second >= end)
        same = here if same is None else same & here
    return same


def partner_of(kind, t):
    if kind == "own":
        return t
    if kind == "core":
        return t + 1 - 2 * lax.rem(t, 2)
    return t - 1 + 2 * lax.rem(t, 2)


def reach_flags(kind, extents, lengths):
    t, h = lax.axis_index("ta"), lax.axis_index("ha")
    count = lax.axis_size("ta")
    other = partner_of(kind, t)
    inside = (other >= 0) & (other < count)
    safe = jnp.clip(other, 0, count - 1)
    near = inside
    if kind != "own":
        near = near & (extents[safe, h, 0] >= 1)
    pairs = [[near & same_clip(2 * safe + i, 2 * t + j, lengths) for j in range(2)] for i in range(2)]
    return pairs, extents[safe, h, 1] >= 1


def any_of(pairs):
    return pairs[0][0] | pairs[0][1] | pairs[1][0] | pairs[1][1]


def column_masks(pairs, tile, valid):
    tiles = len(valid)
    where = lax.broadcasted_iota(jnp.int32, (1, tile * tiles), 1)
    masks = []
    for i in range(2):
        row = None
        for a in range(tiles):
            for j in range(2):
                on = (pairs[i][j] & valid[a]).astype(f32)
                low = a * tile + j * (tile // 2)
                part = jnp.where((where >= low) & (where < low + tile // 2), on, 0.0)
                row = part if row is None else row + part
        masks.append(row)
    return masks


def attend(q, k, v, mask):
    scores = lax.dot_general(q, k, (((1,), (1,)), ((), ())), preferred_element_type=f32)
    weights = (jnp.exp2(scores * (math.log2(math.e) / math.sqrt(hd))) * mask).astype(bf16)
    wide = jnp.concatenate([v, jnp.ones_like(v)], axis=1)
    return jnp.dot(weights, wide, preferred_element_type=f32)


def attend_group(q_ref, k_ref, v_ref, masks, sink):
    half = q_ref.shape[0] // 2
    for b in range(q_ref.shape[1] // hd):
        lanes = slice(b * hd, (b + 1) * hd)
        for i in range(2):
            rows = slice(i * half, (i + 1) * half)
            out = attend(q_ref[rows, lanes], k_ref[:, lanes], v_ref[:, lanes], masks[i])
            sink(b, lanes, rows, out[:, :hd], out[:, hd:])


def lane_id():
    return lax.broadcasted_iota(jnp.int32, (1, hd), 1)


def project_kernel(x_ref, w_ref, gain_ref, q_ref):
    out = jnp.dot(x_ref[...], w_ref[...], preferred_element_type=f32)
    for b in range(out.shape[1] // hd):
        lanes = slice(b * hd, (b + 1) * hd)
        q_ref[:, lanes] = normed(out[:, lanes], gain_ref[...])


def keys_values(x_refs, wk_ref, wv_ref, gain_ref, k_ref, v_ref):
    tile = x_refs[0].shape[0]
    for a, x_ref in enumerate(x_refs):
        rows = slice(a * tile, (a + 1) * tile)
        out = jnp.dot(x_ref[...], wk_ref[...], preferred_element_type=f32)
        for b in range(out.shape[1] // hd):
            lanes = slice(b * hd, (b + 1) * hd)
            k_ref[rows, lanes] = normed(out[:, lanes], gain_ref[...])
        v_ref[rows, :] = jnp.dot(x_ref[...], wv_ref[...], preferred_element_type=f32).astype(bf16)


def add_total(s_ref, head, rows, total):
    s_ref[rows, :] = jnp.where(lane_id() == head, s_ref[rows, :] + total, s_ref[rows, :])


def home_kernel(kind, with_kv, *refs):
    if with_kv:
        ext, lens, q_ref, x_ref, wk_ref, wv_ref, gain_ref, o_ref, s_ref, k_ref, v_ref = refs
        keys_values([x_ref], wk_ref, wv_ref, gain_ref, k_ref, v_ref)
    else:
        ext, lens, q_ref, k_ref, v_ref, o_ref, s_ref = refs
    step = pl.program_id(0)

    @pl.when(step == 0)
    def _():
        s_ref[...] = jnp.zeros_like(s_ref)

    pairs, _ = reach_flags(kind, ext, lens)
    active = any_of(pairs)

    def run():
        masks = column_masks(pairs, q_ref.shape[0], [True])

        def sink(b, lanes, rows, out, total):
            o_ref[rows, lanes] = out
            add_total(s_ref, step * group + b, rows, total)

        attend_group(q_ref, k_ref, v_ref, masks, sink)

    pl.when(active)(run)

    @pl.when(jnp.logical_not(active))
    def _():
        o_ref[...] = jnp.zeros_like(o_ref)


def near_kernel(kind, with_kv, *refs):
    if with_kv:
        ext, lens, q_ref, a_ref, t_ref, xu, xd, wk_ref, wv_ref, gain_ref, o_ref, *outs = refs
        k_ref, v_ref, s_ref = outs
        needed = None
        for other in kinds:
            pairs, reach = reach_flags(other, ext, lens)
            need = any_of(pairs) & reach
            needed = need if needed is None else needed | need

        @pl.when(needed)
        def _():
            keys_values([xu, xd], wk_ref, wv_ref, gain_ref, k_ref, v_ref)
    else:
        ext, lens, q_ref, a_ref, t_ref, k_ref, v_ref, o_ref, s_ref = refs
    step = pl.program_id(0)
    tile, width = q_ref.shape
    back = kind != "own"

    @pl.when(step == 0)
    def _():
        s_ref[...] = t_ref[...]

    pairs, reach = reach_flags(kind, ext, lens)
    active = any_of(pairs) & reach

    def put(rows, start, value):
        if back:
            at = pl.ds(pl.multiple_of(step * width + start, hd), value.shape[1])
            o_ref[rows, at] = value.astype(bf16)
        else:
            o_ref[rows, start : start + value.shape[1]] = value

    @pl.when(active)
    def _():
        h = lax.axis_index("ha")
        masks = column_masks(pairs, tile, [h > 0, h < lax.axis_size("ha") - 1])

        def sink(b, lanes, rows, out, total):
            put(rows, lanes.start, a_ref[rows, lanes] + out)
            add_total(s_ref, step * group + b, rows, total)

        attend_group(q_ref, k_ref, v_ref, masks, sink)

    @pl.when(jnp.logical_not(active))
    def _():
        put(slice(0, tile), 0, a_ref[...])

    if back:

        @pl.when(step == pl.num_programs(0) - 1)
        def _():
            high = s_ref[...].astype(bf16)
            cols = o_ref.shape[1] - 2 * hd
            o_ref[:, cols : cols + hd] = high
            o_ref[:, cols + hd :] = (s_ref[...] - high.astype(f32)).astype(bf16)


def close_kernel(a_ref, t_ref, core_ref, y_ref, w_ref, out_ref, mixed):
    width = a_ref.shape[1]
    total = t_ref[...]
    for ref in (core_ref, y_ref):
        total = total + ref[:, width : width + hd].astype(f32) + ref[:, width + hd :].astype(f32)
    for b in range(width // hd):
        lanes = slice(b * hd, (b + 1) * hd)
        value = a_ref[:, lanes] + core_ref[:, lanes].astype(f32) + y_ref[:, lanes].astype(f32)
        mixed[:, lanes] = (value / total[:, b : b + 1]).astype(bf16)
    out_ref[...] = jnp.dot(mixed[...], w_ref[...], preferred_element_type=f32).astype(bf16)


def whole(shape):
    return pl.BlockSpec(shape, lambda g: (0,) * len(shape))


def by_group(rows, first=0):
    return pl.BlockSpec((rows, group * hd), lambda g: (0, first + g))


def call(kernel, steps, in_specs, out_specs, out_shapes, flops, scratch=()):
    return pl.pallas_call(
        kernel,
        grid=(steps,),
        in_specs=in_specs,
        out_specs=out_specs,
        out_shape=[jax.ShapeDtypeStruct(*shape) for shape in out_shapes],
        scratch_shapes=list(scratch),
        compiler_params=pltpu.CompilerParams(vmem_limit_bytes=vmem_bytes),
        cost_estimate=pl.CostEstimate(flops=int(flops), bytes_accessed=1 << 20, transcendentals=0),
    )


def body(activations, qkv_weight, out_weight, query_gain, key_gain, clip_lengths, extents):
    frames, rows, cols, model = activations.shape
    tile = frames * rows * cols
    inner = out_weight.shape[0]
    steps = inner // (group * hd)
    x = activations.reshape(tile, model)
    q_gain, k_gain = query_gain.reshape(1, hd), key_gain.reshape(1, hd)
    height, time = lax.axis_size("ha"), lax.axis_size("ta")
    smem = pl.BlockSpec(memory_space=pltpu.SMEM)
    up = lax.ppermute(x, "ha", [(i, i + 1) for i in range(height - 1)])
    down = lax.ppermute(x, "ha", [(i + 1, i) for i in range(height - 1)])

    def to_core(a):
        return lax.ppermute(a, "ta", [(i, i ^ 1) for i in range(time)])

    def to_y(a):
        route = [(i, i + 1) for i in range(1, time - 1, 2)]
        return lax.ppermute(a, "ta", route + [(b, a) for a, b in route])

    weight = (model, group * hd)

    def w_spec(part):
        return pl.BlockSpec(weight, lambda g: (0, part * steps + g))

    unit = 2.0 * tile * tile * inner * 4 / 0.9
    mat = 2.0 * tile * model * inner / 0.65
    (q,) = call(
        project_kernel,
        steps,
        [whole((tile, model)), w_spec(0), whole((1, hd))],
        [by_group(tile)],
        [((tile, inner), bf16)],
        mat,
    )(x, qkv_weight, q_gain)
    q_core, q_y = to_core(q), to_y(q)
    flags = [smem, smem]
    kv_specs = [w_spec(1), w_spec(2), whole((1, hd))]
    kv_args = (qkv_weight, qkv_weight, k_gain)
    sum_specs, sum_shapes = (
        [by_group(tile), whole((tile, hd))],
        [((tile, inner), f32), ((tile, hd), f32)],
    )

    def kv_outs(n):
        return [by_group(n * tile)] * 2, [((n * tile, inner), bf16)] * 2

    k_specs, k_shapes = kv_outs(1)
    own, own_total, k_home, v_home = call(
        functools.partial(home_kernel, "own", True),
        steps,
        flags + [by_group(tile), whole((tile, model))] + kv_specs,
        sum_specs + k_specs,
        sum_shapes + k_shapes,
        unit + 2 * mat,
    )(extents, clip_lengths, q, x, *kv_args)

    def at_home(kind, queries):
        return call(
            functools.partial(home_kernel, kind, False),
            steps,
            flags + [by_group(tile)] + k_specs,
            sum_specs,
            sum_shapes,
            unit,
        )(extents, clip_lengths, queries, k_home, v_home)

    core, core_total = at_home("core", q_core)
    y, y_total = at_home("y", q_y)
    near_in = flags + [by_group(tile), by_group(tile), whole((tile, hd))]
    wide = (tile, inner + 2 * hd)
    n_specs, n_shapes = kv_outs(2)
    y_part, k_near, v_near = call(
        functools.partial(near_kernel, "y", True),
        steps,
        near_in + [whole((tile, model))] * 2 + kv_specs,
        [whole(wide)] + n_specs,
        [(wide, bf16)] + n_shapes,
        2 * unit + 4 * mat,
        [pltpu.VMEM((tile, hd), f32)],
    )(extents, clip_lengths, q_y, y, y_total, up, down, *kv_args)
    y_back = to_y(y_part)
    (core_part,) = call(
        functools.partial(near_kernel, "core", False),
        steps,
        near_in + n_specs,
        [whole(wide)],
        [(wide, bf16)],
        2 * unit,
        [pltpu.VMEM((tile, hd), f32)],
    )(extents, clip_lengths, q_core, core, core_total, k_near, v_near)
    core_back = to_core(core_part)
    mine, total = call(
        functools.partial(near_kernel, "own", False),
        steps,
        near_in + n_specs,
        sum_specs,
        sum_shapes,
        2 * unit,
    )(extents, clip_lengths, q, own, own_total, k_near, v_near)
    cut = tile // 4
    (result,) = call(
        close_kernel,
        4,
        [pl.BlockSpec((cut, width), lambda g: (g, 0)) for width in (inner, hd, wide[1], wide[1])]
        + [whole((inner, model))],
        [pl.BlockSpec((cut, model), lambda g: (g, 0))],
        [((tile, model), bf16)],
        mat,
        [pltpu.VMEM((cut, inner), bf16)],
    )(mine, total, core_back, y_back, out_weight)
    return result.reshape(frames, rows, cols, model)


def solution(mesh):
    placed = (P("ta", "ha", None, None), P(), P(), P(), P(), P(), P())
    return jax.shard_map(
        body, mesh=mesh, in_specs=placed, out_specs=P("ta", "ha", None, None), check_vma=False
    )
```

```python
import functools
import math

import jax
import jax.numpy as jnp
from jax import lax
from jax.experimental import pallas as pl
from jax.experimental.pallas import tpu as pltpu
from jax.sharding import PartitionSpec as P

norm_eps = 1e-06
f32 = jnp.float32
bf16 = jnp.bfloat16
hd = 128
group = 4
cost = 2.5
vmem_bytes = 60 << 20


def normed(features, gain):
    mean_sq = jnp.mean(features * features, axis=-1, keepdims=True)
    return (features * lax.rsqrt(mean_sq + norm_eps) * gain).astype(bf16)


def same_clip(first, second, lengths):
    end = 0
    same = None
    for c in range(lengths.shape[0] - 1):
        end = end + lengths[c]
        here = (first >= end) == (second >= end)
        same = here if same is None else same & here
    return same


def core_partner(t):
    return t + 1 - 2 * lax.rem(t, 2)


def y_partner(t):
    return t - 1 + 2 * lax.rem(t, 2)


def itself(t):
    return t


def reach_flags(query_of, key_of, extents, lengths):
    t, h = lax.axis_index("ta"), lax.axis_index("ha")
    count = lax.axis_size("ta")
    query, key = query_of(t), key_of(t)
    inside = (query >= 0) & (query < count) & (key >= 0) & (key < count)
    safe = jnp.clip(query, 0, count - 1)
    near = inside & (jnp.abs(query - key) <= extents[safe, h, 0])
    pairs = [[near & same_clip(2 * safe + i, 2 * key + j, lengths) for j in range(2)] for i in range(2)]
    return pairs, extents[safe, h, 1] >= 1


def any_of(pairs):
    return pairs[0][0] | pairs[0][1] | pairs[1][0] | pairs[1][1]


def home_pieces():
    return [(0, True), (1, True)]


def near_pieces(frames):
    h = lax.axis_index("ha")
    sides = [h > 0, h < lax.axis_size("ha") - 1]
    return [(frame, side) for frame in frames for side in sides]


def column_masks(pairs, half, pieces):
    where = lax.broadcasted_iota(jnp.int32, (1, half * len(pieces)), 1)
    masks = []
    for i in range(2):
        row = None
        for a, (frame, valid) in enumerate(pieces):
            on = (pairs[i][frame] & valid).astype(f32)
            part = jnp.where((where >= a * half) & (where < (a + 1) * half), on, 0.0)
            row = part if row is None else row + part
        masks.append(row)
    return masks


def attend(q, k, v, mask):
    scores = lax.dot_general(q, k, (((1,), (1,)), ((), ())), preferred_element_type=f32)
    weights = (jnp.exp2(scores * (math.log2(math.e) / math.sqrt(hd))) * mask).astype(bf16)
    wide = jnp.concatenate([v, jnp.ones_like(v)], axis=1)
    return jnp.dot(weights, wide, preferred_element_type=f32)


def attend_group(q_ref, kv_refs, pairs, pieces, sink):
    half = q_ref.shape[0] // 2
    masks = column_masks(pairs, half, pieces)
    for b in range(q_ref.shape[1] // hd):
        lanes = slice(b * hd, (b + 1) * hd)
        k = jnp.concatenate([ref[0, :, lanes] for ref in kv_refs], axis=0)
        v = jnp.concatenate([ref[1, :, lanes] for ref in kv_refs], axis=0)
        for i in range(2):
            rows = slice(i * half, (i + 1) * half)
            out = attend(q_ref[rows, lanes], k, v, masks[i])
            sink(b, rows, lanes, out[:, :hd], out[:, hd:])


def lane_id():
    return lax.broadcasted_iota(jnp.int32, (1, hd), 1)


def project_kernel(x_ref, w_ref, gain_ref, q_ref):
    out = jnp.dot(x_ref[...], w_ref[...], preferred_element_type=f32)
    for b in range(out.shape[1] // hd):
        lanes = slice(b * hd, (b + 1) * hd)
        q_ref[:, lanes] = normed(out[:, lanes], gain_ref[...])


def keys_values(x_refs, wk_ref, wv_ref, gain_ref, kv_ref):
    first = 0
    for x_ref in x_refs:
        rows = slice(first, first + x_ref.shape[0])
        first = rows.stop
        out = jnp.dot(x_ref[...], wk_ref[...], preferred_element_type=f32)
        for b in range(out.shape[1] // hd):
            lanes = slice(b * hd, (b + 1) * hd)
            kv_ref[0, rows, lanes] = normed(out[:, lanes], gain_ref[...])
        kv_ref[1, rows, :] = jnp.dot(x_ref[...], wv_ref[...], preferred_element_type=f32).astype(bf16)


def add_total(s_ref, head, rows, total):
    here = (lane_id() & (hd // 2 - 1)) == head
    s_ref[rows, :] = jnp.where(here, s_ref[rows, :] + total, s_ref[rows, :])


def begin(s_ref, t_ref):
    @pl.when(pl.program_id(0) == 0)
    def _():
        s_ref[...] = jnp.zeros_like(s_ref) if t_ref is None else t_ref[...]


def gather(q_ref, a_ref, o_ref, s_ref, choices):
    step = pl.program_id(0)
    taken = None
    for condition, kv_refs, pairs, pieces in choices:
        taken = condition if taken is None else taken | condition

        def run(kv_refs=kv_refs, pairs=pairs, pieces=pieces):
            def sink(b, rows, lanes, out, total):
                o_ref[rows, lanes] = out if a_ref is None else a_ref[rows, lanes] + out
                add_total(s_ref, step * group + b, rows, total)

            attend_group(q_ref, kv_refs, pairs, pieces, sink)

        pl.when(condition)(run)

    @pl.when(jnp.logical_not(taken))
    def _():
        o_ref[...] = jnp.zeros_like(o_ref) if a_ref is None else a_ref[...]


def near_needed(ext, lens):
    needed = None
    for query_of in (itself, core_partner, y_partner):
        pairs, reach = reach_flags(query_of, itself, ext, lens)
        need = any_of(pairs) & reach
        needed = need if needed is None else needed | need
    return needed


def home_kernel(ext, lens, q_ref, x_ref, wk_ref, wv_ref, gain_ref, o_ref, s_ref, kv_ref, late_ref):
    step = pl.program_id(0)
    begin(s_ref, None)
    keys_values([x_ref], wk_ref, wv_ref, gain_ref, kv_ref)
    pairs, _ = reach_flags(itself, itself, ext, lens)
    gather(q_ref, None, o_ref, s_ref, [(any_of(pairs), [kv_ref], pairs, home_pieces())])

    @pl.when(step == 0)
    def _():
        late_ref[...] = x_ref[x_ref.shape[0] // 2 :, :]


def first_kernel(ext, lens, xu, xd, wk_ref, wv_ref, gain_ref, near_ref):
    @pl.when(near_needed(ext, lens))
    def _():
        keys_values([xu, xd], wk_ref, wv_ref, gain_ref, near_ref)


def y_kernel(ext, lens, q_ref, kv_ref, near_ref, o_ref, s_ref):
    begin(s_ref, None)
    pairs, reach = reach_flags(y_partner, itself, ext, lens)
    active = any_of(pairs)
    gather(
        q_ref,
        None,
        o_ref,
        s_ref,
        [
            (active & reach, [kv_ref, near_ref], pairs, home_pieces() + near_pieces([0])),
            (active & jnp.logical_not(reach), [kv_ref], pairs, home_pieces()),
        ],
    )


def second_kernel(
    ext, lens, xu, xd, wk_ref, wv_ref, gain_ref, q_ref, a_ref, t_ref, o_ref, near_ref, s_ref, part
):
    step = pl.program_id(0)
    begin(s_ref, t_ref)

    @pl.when(near_needed(ext, lens))
    def _():
        keys_values([xu, xd], wk_ref, wv_ref, gain_ref, near_ref)

    pairs, reach = reach_flags(y_partner, itself, ext, lens)
    gather(q_ref, a_ref, part, s_ref, [(any_of(pairs) & reach, [near_ref], pairs, near_pieces([1]))])
    width = part.shape[1]
    o_ref[:, pl.ds(pl.multiple_of(step * width, width), width)] = part[...].astype(bf16)

    @pl.when(step == pl.num_programs(0) - 1)
    def _():
        high = s_ref[...].astype(bf16)
        low = (s_ref[...] - high.astype(f32)).astype(bf16)
        o_ref[:, o_ref.shape[1] - hd :] = jnp.where(lane_id() < hd // 2, high, low)


def near_kernel(ext, lens, q_ref, a_ref, t_ref, first_ref, last_ref, o_ref, s_ref):
    begin(s_ref, t_ref)
    pairs, reach = reach_flags(itself, itself, ext, lens)
    keys = [first_ref, last_ref]
    gather(q_ref, a_ref, o_ref, s_ref, [(any_of(pairs) & reach, keys, pairs, near_pieces([0, 1]))])


def core_kernel(ext, lens, q_ref, a_ref, t_ref, home_ref, first_ref, last_ref, o_ref, s_ref):
    begin(s_ref, t_ref)
    pairs, reach = reach_flags(itself, core_partner, ext, lens)
    active = any_of(pairs)
    gather(
        q_ref,
        a_ref,
        o_ref,
        s_ref,
        [
            (active & reach, [home_ref, first_ref, last_ref], pairs, home_pieces() + near_pieces([0, 1])),
            (active & jnp.logical_not(reach), [home_ref], pairs, home_pieces()),
        ],
    )


def close_kernel(a_ref, t_ref, y_ref, w_ref, out_ref, mixed):
    width = a_ref.shape[1]
    back = y_ref[:, width:].astype(f32)
    for b in range(width // hd):
        lanes = slice(b * hd, (b + 1) * hd)
        low = hd // 2 + b
        total = t_ref[:, b : b + 1] + (back[:, b : b + 1] + back[:, low : low + 1])
        value = a_ref[:, lanes] + y_ref[:, lanes].astype(f32)
        mixed[:, lanes] = (value / total).astype(bf16)
    out_ref[...] = jnp.dot(mixed[...], w_ref[...], preferred_element_type=f32).astype(bf16)


def whole(shape):
    return pl.BlockSpec(shape, lambda g: (0,) * len(shape))


def by_group(rows):
    return pl.BlockSpec((rows, group * hd), lambda g: (0, g))


def call(kernel, steps, ins, outs, flops, scratch=(), after=None):
    run, specs, arrays = kernel, [spec for _, spec in ins], [array for array, _ in ins]
    if after is not None:
        place = len(ins)
        specs, arrays = specs + [pl.BlockSpec(memory_space=pl.ANY)], arrays + [after]

        def run(*refs):
            kernel(*refs[:place], *refs[place + 1 :])

    return pl.pallas_call(
        run,
        grid=(steps,),
        in_specs=specs,
        out_specs=[spec for spec, _, _ in outs],
        out_shape=[jax.ShapeDtypeStruct(shape, dtype) for _, shape, dtype in outs],
        scratch_shapes=list(scratch),
        compiler_params=pltpu.CompilerParams(vmem_limit_bytes=vmem_bytes),
        cost_estimate=pl.CostEstimate(flops=int(flops), bytes_accessed=1, transcendentals=0),
    )(*arrays)


def body(activations, qkv_weight, out_weight, query_gain, key_gain, clip_lengths, extents):
    frames, rows, cols, model = activations.shape
    half = rows * cols
    tile = frames * half
    inner = out_weight.shape[0]
    steps = inner // (group * hd)
    x = activations.reshape(tile, model)
    q_gain, k_gain = query_gain.reshape(1, hd), key_gain.reshape(1, hd)
    height, time = lax.axis_size("ha"), lax.axis_size("ta")
    smem = pl.BlockSpec(memory_space=pltpu.SMEM)

    def to_heights(a):
        return (
            lax.ppermute(a, "ha", [(i, i + 1) for i in range(height - 1)]),
            lax.ppermute(a, "ha", [(i + 1, i) for i in range(height - 1)]),
        )

    def to_core(a):
        return lax.ppermute(a, "ta", [(i, i ^ 1) for i in range(time)])

    def to_y(a):
        route = [(i, i + 1) for i in range(1, time - 1, 2)]
        return lax.ppermute(a, "ta", route + [(b, a) for a, b in route])

    def w_of(part):
        return (qkv_weight, pl.BlockSpec((model, group * hd), lambda g: (0, part * steps + g)))

    unit = cost * 2.0 * tile * tile * inner
    mat = cost * 2.0 * tile * model * inner
    total_spec = whole((tile, hd))
    sums = [(by_group(tile), (tile, inner), f32), (total_spec, (tile, hd), f32)]
    kv_spec = pl.BlockSpec((2, tile, group * hd), lambda g: (0, 0, g))
    kv_out = (kv_spec, (2, tile, inner), bf16)
    flags = [(extents, smem), (clip_lengths, smem)]
    kv_weights = [w_of(1), w_of(2), (k_gain, whole((1, hd)))]

    up_first, down_first = to_heights(activations[0].reshape(half, model))
    (q,) = call(
        project_kernel,
        steps,
        [(x, whole((tile, model))), w_of(0), (q_gain, whole((1, hd)))],
        [(by_group(tile), (tile, inner), bf16)],
        mat,
    )
    q_y = to_y(q)
    own, own_total, kv_home, late = call(
        home_kernel,
        steps,
        flags + [(q, by_group(tile)), (x, whole((tile, model)))] + kv_weights,
        sums + [kv_out, (whole((half, model)), (half, model), bf16)],
        unit + 2 * mat,
    )
    up_last, down_last = to_heights(late)
    kv_core = to_core(kv_home)

    def partial(acc, total):
        return [(acc, by_group(tile)), (total, total_spec)]

    def neighbours(up, down):
        return [(up, whole((half, model))), (down, whole((half, model)))]

    (near_first,) = call(
        first_kernel,
        steps,
        flags + neighbours(up_first, down_first) + kv_weights,
        [kv_out],
        2 * mat,
        after=own_total,
    )
    near_first_core = to_core(near_first)
    y, y_total = call(
        y_kernel,
        steps,
        flags + [(q_y, by_group(tile)), (kv_home, kv_spec), (near_first, kv_spec)],
        sums,
        2 * unit,
    )
    wide = (tile, inner + hd)
    y_part, near_last = call(
        second_kernel,
        steps,
        flags + neighbours(up_last, down_last) + kv_weights + [(q_y, by_group(tile))] + partial(y, y_total),
        [(whole(wide), wide, bf16), kv_out],
        unit + 2 * mat,
        [pltpu.VMEM((tile, hd), f32), pltpu.VMEM((tile, group * hd), f32)],
    )
    y_back = to_y(y_part)
    near_last_core = to_core(near_last)

    own, own_total = call(
        near_kernel,
        steps,
        flags + [(q, by_group(tile))] + partial(own, own_total) + [(near_first, kv_spec), (near_last, kv_spec)],
        sums,
        2 * unit,
    )
    own, own_total = call(
        core_kernel,
        steps,
        flags
        + [(q, by_group(tile))]
        + partial(own, own_total)
        + [(kv, kv_spec) for kv in (kv_core, near_first_core, near_last_core)],
        sums,
        3 * unit,
    )
    cut = tile // 4
    (result,) = call(
        close_kernel,
        4,
        [(a, pl.BlockSpec((cut, a.shape[1]), lambda g: (g, 0))) for a in (own, own_total, y_back)]
        + [(out_weight, whole((inner, model)))],
        [(pl.BlockSpec((cut, model), lambda g: (g, 0)), (tile, model), bf16)],
        mat,
        [pltpu.VMEM((cut, inner), bf16)],
    )
    return result.reshape(frames, rows, cols, model)


def solution(mesh):
    placed = (P("ta", "ha", None, None), P(), P(), P(), P(), P(), P())
    return jax.shard_map(
        body, mesh=mesh, in_specs=placed, out_specs=P("ta", "ha", None, None), check_vma=False
    )
```

```python
import functools
import math

import jax
import jax.numpy as jnp
from jax import lax
from jax.experimental import pallas as pl
from jax.experimental.pallas import tpu as pltpu
from jax.sharding import PartitionSpec as P

norm_eps = 1e-06
f32 = jnp.float32
bf16 = jnp.bfloat16
hd = 128
group = 4
cost = 2.5
vmem_bytes = 60 << 20


def normed(features, gain):
    mean_sq = jnp.mean(features * features, axis=-1, keepdims=True)
    return (features * lax.rsqrt(mean_sq + norm_eps) * gain).astype(bf16)


def same_clip(first, second, lengths):
    end = 0
    same = None
    for c in range(lengths.shape[0] - 1):
        end = end + lengths[c]
        here = (first >= end) == (second >= end)
        same = here if same is None else same & here
    return same


def core_partner(t):
    return t + 1 - 2 * lax.rem(t, 2)


def y_partner(t):
    return t - 1 + 2 * lax.rem(t, 2)


def itself(t):
    return t


def reach_flags(query_of, key_of, extents, lengths):
    t, h = lax.axis_index("ta"), lax.axis_index("ha")
    count = lax.axis_size("ta")
    query, key = query_of(t), key_of(t)
    inside = (query >= 0) & (query < count) & (key >= 0) & (key < count)
    safe = jnp.clip(query, 0, count - 1)
    near = inside & (jnp.abs(query - key) <= extents[safe, h, 0])
    pairs = [[near & same_clip(2 * safe + i, 2 * key + j, lengths) for j in range(2)] for i in range(2)]
    return pairs, extents[safe, h, 1] >= 1


def any_of(pairs):
    return pairs[0][0] | pairs[0][1] | pairs[1][0] | pairs[1][1]


def home_pieces():
    return [(0, True), (1, True)]


def near_pieces(frames):
    h = lax.axis_index("ha")
    return [(frame, side) for frame in frames for side in (h > 0, h < lax.axis_size("ha") - 1)]


def column_masks(pairs, half, pieces):
    where = lax.broadcasted_iota(jnp.int32, (1, half * len(pieces)), 1)
    masks = []
    for i in range(2):
        row = None
        for a, (frame, valid) in enumerate(pieces):
            on = (pairs[i][frame] & valid).astype(f32)
            part = jnp.where((where >= a * half) & (where < (a + 1) * half), on, 0.0)
            row = part if row is None else row + part
        masks.append(row)
    return masks


def attend(q, k, v, mask):
    scores = lax.dot_general(q, k, (((1,), (1,)), ((), ())), preferred_element_type=f32)
    weights = (jnp.exp2(scores * (math.log2(math.e) / math.sqrt(hd))) * mask).astype(bf16)
    wide = jnp.concatenate([v, jnp.ones_like(v)], axis=1)
    return jnp.dot(weights, wide, preferred_element_type=f32)


def attend_group(q_ref, kv_refs, pairs, pieces, sink):
    half = q_ref.shape[0] // 2
    masks = column_masks(pairs, half, pieces)
    for b in range(q_ref.shape[1] // hd):
        lanes = slice(b * hd, (b + 1) * hd)
        k = jnp.concatenate([ref[0, :, lanes] for ref in kv_refs], axis=0)
        v = jnp.concatenate([ref[1, :, lanes] for ref in kv_refs], axis=0)
        for i in range(2):
            rows = slice(i * half, (i + 1) * half)
            out = attend(q_ref[rows, lanes], k, v, masks[i])
            sink(b, rows, lanes, out[:, :hd], out[:, hd:])


def lane_id():
    return lax.broadcasted_iota(jnp.int32, (1, hd), 1)


def project_kernel(x_ref, w_ref, gain_ref, q_ref):
    out = jnp.dot(x_ref[...], w_ref[...], preferred_element_type=f32)
    for b in range(out.shape[1] // hd):
        lanes = slice(b * hd, (b + 1) * hd)
        q_ref[:, lanes] = normed(out[:, lanes], gain_ref[...])


def keys_values(x_refs, wk_ref, wv_ref, gain_ref, kv_ref):
    x = jnp.concatenate([ref[...] for ref in x_refs], axis=0)
    w = jnp.concatenate([wk_ref[...], wv_ref[...]], axis=1)
    out = jnp.dot(x, w, preferred_element_type=f32)
    width = wk_ref.shape[1]
    for b in range(width // hd):
        lanes = slice(b * hd, (b + 1) * hd)
        kv_ref[0, :, lanes] = normed(out[:, lanes], gain_ref[...])
    kv_ref[1] = out[:, width:].astype(bf16)


def add_total(s_ref, head, rows, total):
    here = (lane_id() & (hd // 2 - 1)) == head
    s_ref[rows, :] = jnp.where(here, s_ref[rows, :] + total, s_ref[rows, :])


def begin(s_ref, t_ref):
    @pl.when(pl.program_id(0) == 0)
    def _():
        s_ref[...] = jnp.zeros_like(s_ref) if t_ref is None else t_ref[...]


def gather(q_ref, a_ref, o_ref, s_ref, choices):
    step = pl.program_id(0)
    taken = None
    for condition, kv_refs, pairs, pieces in choices:
        taken = condition if taken is None else taken | condition

        def run(kv_refs=kv_refs, pairs=pairs, pieces=pieces):
            def sink(b, rows, lanes, out, total):
                o_ref[rows, lanes] = out if a_ref is None else a_ref[rows, lanes] + out
                add_total(s_ref, step * group + b, rows, total)

            attend_group(q_ref, kv_refs, pairs, pieces, sink)

        pl.when(condition)(run)

    @pl.when(jnp.logical_not(taken))
    def _():
        o_ref[...] = jnp.zeros_like(o_ref) if a_ref is None else a_ref[...]


def near_needed(ext, lens):
    needed = None
    for query_of in (itself, core_partner, y_partner):
        pairs, reach = reach_flags(query_of, itself, ext, lens)
        need = any_of(pairs) & reach
        needed = need if needed is None else needed | need
    return needed


def home_kernel(ext, lens, q_ref, x_ref, wk_ref, wv_ref, gain_ref, o_ref, s_ref, kv_ref, late_ref):
    begin(s_ref, None)
    keys_values([x_ref], wk_ref, wv_ref, gain_ref, kv_ref)
    pairs, _ = reach_flags(itself, itself, ext, lens)
    gather(q_ref, None, o_ref, s_ref, [(any_of(pairs), [kv_ref], pairs, home_pieces())])

    @pl.when(pl.program_id(0) == 0)
    def _():
        late_ref[...] = x_ref[x_ref.shape[0] // 2 :, :]


def first_kernel(ext, lens, xu, xd, wk_ref, wv_ref, gain_ref, q_ref, kv_ref, o_ref, s_ref, near_ref):
    begin(s_ref, None)

    @pl.when(near_needed(ext, lens))
    def _():
        keys_values([xu, xd], wk_ref, wv_ref, gain_ref, near_ref)

    pairs, reach = reach_flags(y_partner, itself, ext, lens)
    active = any_of(pairs)
    gather(
        q_ref,
        None,
        o_ref,
        s_ref,
        [
            (active & reach, [kv_ref, near_ref], pairs, home_pieces() + near_pieces([0])),
            (active & jnp.logical_not(reach), [kv_ref], pairs, home_pieces()),
        ],
    )


def second_kernel(
    ext, lens, xu, xd, wk_ref, wv_ref, gain_ref, q_ref, a_ref, t_ref, o_ref, near_ref, s_ref, part
):
    step = pl.program_id(0)
    begin(s_ref, t_ref)

    @pl.when(near_needed(ext, lens))
    def _():
        keys_values([xu, xd], wk_ref, wv_ref, gain_ref, near_ref)

    pairs, reach = reach_flags(y_partner, itself, ext, lens)
    gather(q_ref, a_ref, part, s_ref, [(any_of(pairs) & reach, [near_ref], pairs, near_pieces([1]))])
    width = part.shape[1]
    o_ref[:, pl.ds(pl.multiple_of(step * width, width), width)] = part[...].astype(bf16)

    @pl.when(step == pl.num_programs(0) - 1)
    def _():
        high = s_ref[...].astype(bf16)
        low = (s_ref[...] - high.astype(f32)).astype(bf16)
        o_ref[:, o_ref.shape[1] - hd :] = jnp.where(lane_id() < hd // 2, high, low)


def own_kernel(ext, lens, q_ref, a_ref, t_ref, n0_ref, n1_ref, core_ref, o_ref, s_ref):
    begin(s_ref, t_ref)
    pairs, reach = reach_flags(itself, itself, ext, lens)
    near = near_pieces([0, 1])
    gather(q_ref, a_ref, o_ref, s_ref, [(any_of(pairs) & reach, [n0_ref, n1_ref], pairs, near)])
    pairs, _ = reach_flags(itself, core_partner, ext, lens)
    gather(q_ref, o_ref, o_ref, s_ref, [(any_of(pairs), [core_ref], pairs, home_pieces())])


def core_kernel(ext, lens, q_ref, a_ref, t_ref, c0_ref, c1_ref, o_ref, s_ref, part):
    begin(s_ref, t_ref)
    pairs, reach = reach_flags(itself, core_partner, ext, lens)
    near = near_pieces([0, 1])
    gather(q_ref, a_ref, part, s_ref, [(any_of(pairs) & reach, [c0_ref, c1_ref], pairs, near)])
    o_ref[...] = part[...].astype(bf16)


def close_kernel(a_ref, t_ref, y_ref, back_ref, w_ref, out_ref, total):
    step = pl.program_id(0)
    count = a_ref.shape[1] // hd
    low = back_ref[...].astype(f32)
    sums = t_ref[...] + (low + pltpu.roll(low, hd // 2, 1))
    values = []
    for b in range(count):
        lanes = slice(b * hd, (b + 1) * hd)
        sum_b = jnp.sum(jnp.where(lane_id() == step * count + b, sums, 0.0), axis=1, keepdims=True)
        value = a_ref[:, lanes].astype(f32) + y_ref[:, lanes].astype(f32)
        values.append((value / sum_b).astype(bf16))
    mixed = values[0] if count == 1 else jnp.concatenate(values, axis=1)
    part = jnp.dot(mixed, w_ref[...], preferred_element_type=f32)

    @pl.when(step == 0)
    def _():
        total[...] = part

    @pl.when((step > 0) & (step < pl.num_programs(0) - 1))
    def _():
        total[...] += part

    @pl.when(step == pl.num_programs(0) - 1)
    def _():
        out_ref[...] = (total[...] + part).astype(bf16)


def whole(shape):
    return pl.BlockSpec(shape, lambda g: (0,) * len(shape), pipeline_mode=pl.Buffered(1))


def by_group(rows):
    return pl.BlockSpec((rows, group * hd), lambda g: (0, g))


def call(kernel, steps, ins, outs, flops, scratch=(), after=None):
    run, specs, arrays = kernel, [spec for _, spec in ins], [array for array, _ in ins]
    if after is not None:
        place = len(ins)
        specs, arrays = specs + [pl.BlockSpec(memory_space=pl.ANY)], arrays + [after]

        def run(*refs):
            kernel(*refs[:place], *refs[place + 1 :])

    return pl.pallas_call(
        run,
        grid=(steps,),
        in_specs=specs,
        out_specs=[spec for spec, _, _ in outs],
        out_shape=[jax.ShapeDtypeStruct(shape, dtype) for _, shape, dtype in outs],
        scratch_shapes=list(scratch),
        compiler_params=pltpu.CompilerParams(vmem_limit_bytes=vmem_bytes),
        cost_estimate=pl.CostEstimate(flops=int(flops), bytes_accessed=1, transcendentals=0),
    )(*arrays)


def body(activations, qkv_weight, out_weight, query_gain, key_gain, clip_lengths, extents):
    frames, rows, cols, model = activations.shape
    half = rows * cols
    tile = frames * half
    inner = out_weight.shape[0]
    steps = inner // (group * hd)
    x = activations.reshape(tile, model)
    q_gain, k_gain = query_gain.reshape(1, hd), key_gain.reshape(1, hd)
    height, time = lax.axis_size("ha"), lax.axis_size("ta")
    smem = pl.BlockSpec(memory_space=pltpu.SMEM)

    def to_heights(a):
        return (
            lax.ppermute(a, "ha", [(i, i + 1) for i in range(height - 1)]),
            lax.ppermute(a, "ha", [(i + 1, i) for i in range(height - 1)]),
        )

    def to_core(a):
        return lax.ppermute(a, "ta", [(i, i ^ 1) for i in range(time)])

    def to_y(a):
        route = [(i, i + 1) for i in range(1, time - 1, 2)]
        return lax.ppermute(a, "ta", route + [(b, a) for a, b in route])

    def w_of(part):
        return (qkv_weight, pl.BlockSpec((model, group * hd), lambda g: (0, part * steps + g)))

    unit = cost * 2.0 * tile * tile * inner
    mat = cost * 2.0 * tile * model * inner
    total_spec = whole((tile, hd))
    sums = [(by_group(tile), (tile, inner), f32), (total_spec, (tile, hd), f32)]
    kv_spec = pl.BlockSpec((2, tile, group * hd), lambda g: (0, 0, g))
    kv_out = (kv_spec, (2, tile, inner), bf16)
    flags = [(extents, smem), (clip_lengths, smem)]
    kv_weights = [w_of(1), w_of(2), (k_gain, whole((1, hd)))]

    def partial(acc, total):
        return [(acc, by_group(tile)), (total, total_spec)]

    up_first, down_first = to_heights(activations[0].reshape(half, model))
    (q,) = call(
        project_kernel,
        steps,
        [(x, whole((tile, model))), w_of(0), (q_gain, whole((1, hd)))],
        [(by_group(tile), (tile, inner), bf16)],
        mat,
    )
    q_y = to_y(q)
    own, own_total, kv_home, late = call(
        home_kernel,
        steps,
        flags + [(q, by_group(tile)), (x, whole((tile, model)))] + kv_weights,
        sums + [kv_out, (whole((half, model)), (half, model), bf16)],
        unit + 2 * mat,
    )
    up_last, down_last = to_heights(late)
    kv_core = to_core(kv_home)

    def neighbours(up, down):
        return [(up, whole((half, model))), (down, whole((half, model)))]

    y, y_total, near_first = call(
        first_kernel,
        steps,
        flags + neighbours(up_first, down_first) + kv_weights + [(q_y, by_group(tile)), (kv_home, kv_spec)],
        sums + [kv_out],
        2 * unit + 2 * mat,
        after=own_total,
    )
    near_first_core = to_core(near_first)
    wide = (tile, inner + hd)
    y_part, near_last = call(
        second_kernel,
        steps,
        flags + neighbours(up_last, down_last) + kv_weights + [(q_y, by_group(tile))] + partial(y, y_total),
        [(whole(wide), wide, bf16), kv_out],
        unit + 2 * mat,
        [pltpu.VMEM((tile, hd), f32), pltpu.VMEM((tile, group * hd), f32)],
    )
    y_back = to_y(y_part)
    near_last_core = to_core(near_last)
    own, own_total = call(
        own_kernel,
        steps,
        flags
        + [(q, by_group(tile))]
        + partial(own, own_total)
        + [(kv, kv_spec) for kv in (near_first, near_last, kv_core)],
        sums,
        3 * unit,
    )
    own, own_total = call(
        core_kernel,
        steps,
        flags
        + [(q, by_group(tile))]
        + partial(own, own_total)
        + [(kv, kv_spec) for kv in (near_first_core, near_last_core)],
        [(by_group(tile), (tile, inner), bf16), sums[1]],
        2 * unit,
        [pltpu.VMEM((tile, group * hd), f32)],
    )
    heads = 2
    close_spec = pl.BlockSpec((tile, heads * hd), lambda g: (0, g))
    (result,) = call(
        close_kernel,
        inner // (heads * hd),
        [
            (own, close_spec),
            (own_total, total_spec),
            (y_back, close_spec),
            (y_back, pl.BlockSpec((tile, hd), lambda g: (0, inner // hd))),
            (out_weight, pl.BlockSpec((heads * hd, model), lambda g: (g, 0))),
        ],
        [(whole((tile, model)), (tile, model), bf16)],
        mat,
        [pltpu.VMEM((tile, model), f32)],
    )
    return result.reshape(frames, rows, cols, model)


def solution(mesh):
    placed = (P("ta", "ha", None, None), P(), P(), P(), P(), P(), P())
    return jax.shard_map(
        body, mesh=mesh, in_specs=placed, out_specs=P("ta", "ha", None, None), check_vma=False
    )
```

```python
import functools
import math

import jax
import jax.numpy as jnp
from jax import lax
from jax.experimental import pallas as pl
from jax.experimental.pallas import tpu as pltpu
from jax.sharding import PartitionSpec as P

norm_eps = 1e-06
f32 = jnp.float32
bf16 = jnp.bfloat16
hd = 128
group = 4
cost = 2.5
close_steps = 5
vmem_weights = 50 << 20
vmem_other = 20 << 20


def normed(features, gain):
    mean_sq = jnp.mean(features * features, axis=-1, keepdims=True)
    return (features * lax.rsqrt(mean_sq + norm_eps) * gain).astype(bf16)


def same_clip(first, second, lengths):
    end = 0
    same = None
    for c in range(lengths.shape[0] - 1):
        end = end + lengths[c]
        here = (first >= end) == (second >= end)
        same = here if same is None else same & here
    return same


def core_partner(t):
    return t + 1 - 2 * lax.rem(t, 2)


def y_partner(t):
    return t - 1 + 2 * lax.rem(t, 2)


def itself(t):
    return t


def reach_flags(query_of, key_of, extents, lengths):
    t, h = lax.axis_index("ta"), lax.axis_index("ha")
    count = lax.axis_size("ta")
    query, key = query_of(t), key_of(t)
    inside = (query >= 0) & (query < count) & (key >= 0) & (key < count)
    safe = jnp.clip(query, 0, count - 1)
    near = inside & (jnp.abs(query - key) <= extents[safe, h, 0])
    pairs = [[near & same_clip(2 * safe + i, 2 * key + j, lengths) for j in range(2)] for i in range(2)]
    return pairs, extents[safe, h, 1] >= 1


def any_of(pairs):
    return pairs[0][0] | pairs[0][1] | pairs[1][0] | pairs[1][1]


def home_pieces():
    return [(0, True), (1, True)]


def near_pieces(frames):
    h = lax.axis_index("ha")
    both = (h > 0) & (h < lax.axis_size("ha") - 1)
    return [(frame, side) for frame in frames for side in (True, both)]


def column_masks(pairs, half, pieces):
    where = lax.broadcasted_iota(jnp.int32, (1, half * len(pieces)), 1)
    masks = []
    for i in range(2):
        row = None
        for a, (frame, valid) in enumerate(pieces):
            on = (pairs[i][frame] & valid).astype(f32)
            part = jnp.where((where >= a * half) & (where < (a + 1) * half), on, 0.0)
            row = part if row is None else row + part
        masks.append(row)
    return masks


def attend(q, k, v, mask):
    scores = lax.dot_general(q, k, (((1,), (1,)), ((), ())), preferred_element_type=f32)
    weights = (jnp.exp2(scores * (math.log2(math.e) / math.sqrt(hd))) * mask).astype(bf16)
    wide = jnp.concatenate([v, jnp.ones_like(v)], axis=1)
    return jnp.dot(weights, wide, preferred_element_type=f32)


def attend_group(q_ref, kv_refs, pairs, pieces, sink):
    half = q_ref.shape[0] // 2
    masks = column_masks(pairs, half, pieces)
    for b in range(q_ref.shape[1] // hd):
        lanes = slice(b * hd, (b + 1) * hd)
        k = jnp.concatenate([ref[0, :, lanes] for ref in kv_refs], axis=0)
        v = jnp.concatenate([ref[1, :, lanes] for ref in kv_refs], axis=0)
        for i in range(2):
            rows = slice(i * half, (i + 1) * half)
            out = attend(q_ref[rows, lanes], k, v, masks[i])
            sink(b, rows, lanes, out[:, :hd], out[:, hd:])


def lane_id():
    return lax.broadcasted_iota(jnp.int32, (1, hd), 1)


def project_kernel(x_ref, w_ref, gain_ref, q_ref):
    out = jnp.dot(x_ref[...], w_ref[...], preferred_element_type=f32)
    for b in range(out.shape[1] // hd):
        lanes = slice(b * hd, (b + 1) * hd)
        q_ref[:, lanes] = normed(out[:, lanes], gain_ref[...])


def keys_values(x_refs, wk_ref, wv_ref, gain_ref, kv_ref):
    x = x_refs[0][...] if len(x_refs) == 1 else jnp.concatenate([ref[...] for ref in x_refs], axis=0)
    w = jnp.concatenate([wk_ref[...], wv_ref[...]], axis=1)
    out = jnp.dot(x, w, preferred_element_type=f32)
    width = wk_ref.shape[1]
    for b in range(width // hd):
        lanes = slice(b * hd, (b + 1) * hd)
        kv_ref[0, :, lanes] = normed(out[:, lanes], gain_ref[...])
    kv_ref[1] = out[:, width:].astype(bf16)


def add_total(s_ref, head, rows, total):
    here = (lane_id() & (hd // 2 - 1)) == head
    s_ref[rows, :] = jnp.where(here, s_ref[rows, :] + total, s_ref[rows, :])


def begin(s_ref, t_ref):
    @pl.when(pl.program_id(0) == 0)
    def _():
        s_ref[...] = jnp.zeros_like(s_ref) if t_ref is None else t_ref[...]


def gather(q_ref, a_ref, o_ref, s_ref, choices):
    step = pl.program_id(0)
    taken = None
    for condition, kv_refs, pairs, pieces in choices:
        taken = condition if taken is None else taken | condition

        def run(kv_refs=kv_refs, pairs=pairs, pieces=pieces):
            def sink(b, rows, lanes, out, total):
                o_ref[rows, lanes] = out if a_ref is None else a_ref[rows, lanes] + out
                add_total(s_ref, step * group + b, rows, total)

            attend_group(q_ref, kv_refs, pairs, pieces, sink)

        pl.when(condition)(run)

    @pl.when(jnp.logical_not(taken))
    def _():
        o_ref[...] = jnp.zeros_like(o_ref) if a_ref is None else a_ref[...]


def near_needed(ext, lens):
    needed = None
    for query_of in (itself, core_partner, y_partner):
        pairs, reach = reach_flags(query_of, itself, ext, lens)
        need = any_of(pairs) & reach
        needed = need if needed is None else needed | need
    return needed


def home_kernel(ext, lens, q_ref, x_ref, wk_ref, wv_ref, gain_ref, o_ref, s_ref, kv_ref, late_ref):
    step = pl.program_id(0)
    begin(s_ref, None)
    keys_values([x_ref], wk_ref, wv_ref, gain_ref, kv_ref)
    pairs, _ = reach_flags(itself, itself, ext, lens)
    gather(q_ref, None, o_ref, s_ref, [(any_of(pairs), [kv_ref], pairs, home_pieces())])

    @pl.when(step == 0)
    def _():
        late_ref[...] = x_ref[x_ref.shape[0] // 2 :, :]


def first_kernel(ext, lens, xu, xd, wk_ref, wv_ref, gain_ref, near_ref):
    @pl.when(near_needed(ext, lens))
    def _():
        keys_values([xu, xd], wk_ref, wv_ref, gain_ref, near_ref)


def y_kernel(ext, lens, q_ref, kv_ref, near_ref, o_ref, s_ref):
    begin(s_ref, None)
    pairs, reach = reach_flags(y_partner, itself, ext, lens)
    active = any_of(pairs)
    gather(
        q_ref,
        None,
        o_ref,
        s_ref,
        [
            (active & reach, [kv_ref, near_ref], pairs, home_pieces() + near_pieces([0])),
            (active & jnp.logical_not(reach), [kv_ref], pairs, home_pieces()),
        ],
    )


def second_kernel(
    ext, lens, xu, xd, wk_ref, wv_ref, gain_ref, q_ref, a_ref, t_ref, o_ref, near_ref, s_ref, part
):
    step = pl.program_id(0)
    begin(s_ref, t_ref)

    @pl.when(near_needed(ext, lens))
    def _():
        keys_values([xu, xd], wk_ref, wv_ref, gain_ref, near_ref)

    pairs, reach = reach_flags(y_partner, itself, ext, lens)
    gather(q_ref, a_ref, part, s_ref, [(any_of(pairs) & reach, [near_ref], pairs, near_pieces([1]))])
    width = part.shape[1]
    o_ref[:, pl.ds(pl.multiple_of(step * width, width), width)] = part[...].astype(bf16)

    @pl.when(step == pl.num_programs(0) - 1)
    def _():
        high = s_ref[...].astype(bf16)
        low = (s_ref[...] - high.astype(f32)).astype(bf16)
        o_ref[:, o_ref.shape[1] - hd :] = jnp.where(lane_id() < hd // 2, high, low)


def near_kernel(ext, lens, q_ref, a_ref, t_ref, first_ref, last_ref, o_ref, s_ref):
    begin(s_ref, t_ref)
    pairs, reach = reach_flags(itself, itself, ext, lens)
    keys = [first_ref, last_ref]
    gather(q_ref, a_ref, o_ref, s_ref, [(any_of(pairs) & reach, keys, pairs, near_pieces([0, 1]))])


def core_kernel(ext, lens, q_ref, a_ref, t_ref, home_ref, first_ref, last_ref, o_ref, s_ref, part):
    begin(s_ref, t_ref)
    pairs, reach = reach_flags(itself, core_partner, ext, lens)
    active = any_of(pairs)
    gather(
        q_ref,
        a_ref,
        part,
        s_ref,
        [
            (active & reach, [home_ref, first_ref, last_ref], pairs, home_pieces() + near_pieces([0, 1])),
            (active & jnp.logical_not(reach), [home_ref], pairs, home_pieces()),
        ],
    )
    o_ref[...] = part[...].astype(bf16)


def close_kernel(a_ref, t_ref, y_ref, w_ref, out_ref, mixed):
    width = a_ref.shape[1]
    back = y_ref[:, width:].astype(f32)
    for b in range(width // hd):
        lanes = slice(b * hd, (b + 1) * hd)
        low = hd // 2 + b
        total = t_ref[:, b : b + 1] + (back[:, b : b + 1] + back[:, low : low + 1])
        value = a_ref[:, lanes].astype(f32) + y_ref[:, lanes].astype(f32)
        mixed[:, lanes] = (value / total).astype(bf16)
    out_ref[...] = jnp.dot(mixed[...], w_ref[...], preferred_element_type=f32).astype(bf16)


def whole(shape):
    return pl.BlockSpec(shape, lambda g: (0,) * len(shape), pipeline_mode=pl.Buffered(1))


def by_group(rows):
    return pl.BlockSpec((rows, group * hd), lambda g: (0, g))


def call(kernel, steps, ins, outs, flops, scratch=(), after=None, vmem=vmem_other):
    run, specs, arrays = kernel, [spec for _, spec in ins], [array for array, _ in ins]
    if after is not None:
        place = len(ins)
        specs, arrays = specs + [pl.BlockSpec(memory_space=pl.ANY)], arrays + [after]

        def run(*refs):
            kernel(*refs[:place], *refs[place + 1 :])

    return pl.pallas_call(
        run,
        grid=(steps,),
        in_specs=specs,
        out_specs=[spec for spec, _, _ in outs],
        out_shape=[jax.ShapeDtypeStruct(shape, dtype) for _, shape, dtype in outs],
        scratch_shapes=list(scratch),
        compiler_params=pltpu.CompilerParams(vmem_limit_bytes=vmem),
        cost_estimate=pl.CostEstimate(flops=int(flops), bytes_accessed=1, transcendentals=0),
    )(*arrays)


def body(activations, qkv_weight, out_weight, query_gain, key_gain, clip_lengths, extents):
    frames, rows, cols, model = activations.shape
    half = rows * cols
    tile = frames * half
    inner = out_weight.shape[0]
    steps = inner // (group * hd)
    x = activations.reshape(tile, model)
    q_gain, k_gain = query_gain.reshape(1, hd), key_gain.reshape(1, hd)
    smem = pl.BlockSpec(memory_space=pltpu.SMEM)

    def swap(a, axis, first):
        route = [(i, i + 1) for i in range(first, lax.axis_size(axis) - 1, 2)]
        return lax.ppermute(a, axis, route + [(j, i) for i, j in route])

    def to_heights(a):
        return swap(a, "ha", 0), swap(a, "ha", 1)

    def to_core(a):
        return swap(a, "ta", 0)

    def to_y(a):
        return swap(a, "ta", 1)

    def w_of(part):
        return (qkv_weight, pl.BlockSpec((model, group * hd), lambda g: (0, part * steps + g)))

    unit = cost * 2.0 * tile * tile * inner
    mat = cost * 2.0 * tile * model * inner
    total_spec = whole((tile, hd))
    sums = [(by_group(tile), (tile, inner), f32), (total_spec, (tile, hd), f32)]
    kv_spec = pl.BlockSpec((2, tile, group * hd), lambda g: (0, 0, g))
    kv_out = (kv_spec, (2, tile, inner), bf16)
    flags = [(extents, smem), (clip_lengths, smem)]
    kv_weights = [w_of(1), w_of(2), (k_gain, whole((1, hd)))]

    up_first, down_first = to_heights(activations[0].reshape(half, model))
    (q,) = call(
        project_kernel,
        steps,
        [(x, whole((tile, model))), w_of(0), (q_gain, whole((1, hd)))],
        [(by_group(tile), (tile, inner), bf16)],
        mat,
        vmem=vmem_weights,
    )
    q_y = to_y(q)
    own, own_total, kv_home, late = call(
        home_kernel,
        steps,
        flags + [(q, by_group(tile)), (x, whole((tile, model)))] + kv_weights,
        sums + [kv_out, (whole((half, model)), (half, model), bf16)],
        unit + 2 * mat,
        vmem=vmem_weights,
    )
    up_last, down_last = to_heights(late)
    kv_core = to_core(kv_home)

    def partial(acc, total):
        return [(acc, by_group(tile)), (total, total_spec)]

    def neighbours(up, down):
        return [(up, whole((half, model))), (down, whole((half, model)))]

    (near_first,) = call(
        first_kernel,
        steps,
        flags + neighbours(up_first, down_first) + kv_weights,
        [kv_out],
        2 * mat,
        after=own_total,
        vmem=vmem_weights,
    )
    near_first_core = to_core(near_first)
    y, y_total = call(
        y_kernel,
        steps,
        flags + [(q_y, by_group(tile)), (kv_home, kv_spec), (near_first, kv_spec)],
        sums,
        2 * unit,
    )
    wide = (tile, inner + hd)
    y_part, near_last = call(
        second_kernel,
        steps,
        flags + neighbours(up_last, down_last) + kv_weights + [(q_y, by_group(tile))] + partial(y, y_total),
        [(whole(wide), wide, bf16), kv_out],
        unit + 2 * mat,
        [pltpu.VMEM((tile, hd), f32), pltpu.VMEM((tile, group * hd), f32)],        vmem=vmem_weights,
    )
    y_back = to_y(y_part)
    near_last_core = to_core(near_last)

    own, own_total = call(
        near_kernel,
        steps,
        flags + [(q, by_group(tile))] + partial(own, own_total) + [(near_first, kv_spec), (near_last, kv_spec)],
        sums,
        2 * unit,
    )
    own, own_total = call(
        core_kernel,
        steps,
        flags
        + [(q, by_group(tile))]
        + partial(own, own_total)
        + [(kv, kv_spec) for kv in (kv_core, near_first_core, near_last_core)],
        [(by_group(tile), (tile, inner), bf16), sums[1]],
        3 * unit,
        [pltpu.VMEM((tile, group * hd), f32)],
    )
    cut = tile // close_steps
    (result,) = call(
        close_kernel,
        close_steps,
        [(a, pl.BlockSpec((cut, a.shape[1]), lambda g: (g, 0))) for a in (own, own_total, y_back)]
        + [(out_weight, whole((inner, model)))],
        [(pl.BlockSpec((cut, model), lambda g: (g, 0)), (tile, model), bf16)],
        mat,
        [pltpu.VMEM((cut, inner), bf16)],
    )
    return result.reshape(frames, rows, cols, model)


def solution(mesh):
    placed = (P("ta", "ha", None, None), P(), P(), P(), P(), P(), P())
    return jax.shard_map(
        body, mesh=mesh, in_specs=placed, out_specs=P("ta", "ha", None, None), check_vma=False
    )
```

```python
import functools
import math

import jax
import jax.numpy as jnp
from jax import lax
from jax.experimental import pallas as pl
from jax.experimental.pallas import tpu as pltpu
from jax.sharding import PartitionSpec as P

norm_eps = 1e-06
f32 = jnp.float32
bf16 = jnp.bfloat16
hd = 128
group = 4
cost = 2.5
close_steps = 5
vmem_weights = 50 << 20
vmem_other = 20 << 20


def normed(features, gain):
    mean_sq = jnp.mean(features * features, axis=-1, keepdims=True)
    return (features * lax.rsqrt(mean_sq + norm_eps) * gain).astype(bf16)


def same_clip(first, second, lengths):
    end = 0
    same = None
    for c in range(lengths.shape[0] - 1):
        end = end + lengths[c]
        here = (first >= end) == (second >= end)
        same = here if same is None else same & here
    return same


def core_partner(t):
    return t + 1 - 2 * lax.rem(t, 2)


def y_partner(t):
    return t - 1 + 2 * lax.rem(t, 2)


def itself(t):
    return t


def reach_flags(query_of, key_of, extents, lengths):
    t, h = lax.axis_index("ta"), lax.axis_index("ha")
    count = lax.axis_size("ta")
    query, key = query_of(t), key_of(t)
    inside = (query >= 0) & (query < count) & (key >= 0) & (key < count)
    safe = jnp.clip(query, 0, count - 1)
    near = inside & (jnp.abs(query - key) <= extents[safe, h, 0])
    pairs = [[near & same_clip(2 * safe + i, 2 * key + j, lengths) for j in range(2)] for i in range(2)]
    return pairs, extents[safe, h, 1] >= 1


def any_of(pairs):
    return pairs[0][0] | pairs[0][1] | pairs[1][0] | pairs[1][1]


def home_pieces():
    return [(0, True), (1, True)]


def near_pieces(frames):
    h = lax.axis_index("ha")
    both = (h > 0) & (h < lax.axis_size("ha") - 1)
    return [(frame, side) for frame in frames for side in (True, both)]


def column_masks(pairs, half, pieces):
    where = lax.broadcasted_iota(jnp.int32, (1, half * len(pieces)), 1)
    masks = []
    for i in range(2):
        row = None
        for a, (frame, valid) in enumerate(pieces):
            on = (pairs[i][frame] & valid).astype(f32)
            part = jnp.where((where >= a * half) & (where < (a + 1) * half), on, 0.0)
            row = part if row is None else row + part
        masks.append(row)
    return masks


def attend(q, k, v, mask):
    scores = lax.dot_general(q, k, (((1,), (1,)), ((), ())), preferred_element_type=f32)
    weights = (jnp.exp2(scores * (math.log2(math.e) / math.sqrt(hd))) * mask).astype(bf16)
    wide = jnp.concatenate([v, jnp.ones_like(v)], axis=1)
    return jnp.dot(weights, wide, preferred_element_type=f32)


def attend_group(q_ref, kv_refs, pairs, pieces, sink):
    half = q_ref.shape[0] // 2
    masks = column_masks(pairs, half, pieces)
    for b in range(q_ref.shape[1] // hd):
        lanes = slice(b * hd, (b + 1) * hd)
        k = jnp.concatenate([ref[0, :, lanes] for ref in kv_refs], axis=0)
        v = jnp.concatenate([ref[1, :, lanes] for ref in kv_refs], axis=0)
        for i in range(2):
            rows = slice(i * half, (i + 1) * half)
            out = attend(q_ref[rows, lanes], k, v, masks[i])
            sink(b, rows, lanes, out[:, :hd], out[:, hd:])


def lane_id():
    return lax.broadcasted_iota(jnp.int32, (1, hd), 1)


def project_kernel(x_ref, w_ref, gain_ref, q_ref):
    out = jnp.dot(x_ref[...], w_ref[...], preferred_element_type=f32)
    for b in range(out.shape[1] // hd):
        lanes = slice(b * hd, (b + 1) * hd)
        q_ref[:, lanes] = normed(out[:, lanes], gain_ref[...])


def keys_values(x_refs, wk_ref, wv_ref, gain_ref, kv_ref):
    x = x_refs[0][...] if len(x_refs) == 1 else jnp.concatenate([ref[...] for ref in x_refs], axis=0)
    w = jnp.concatenate([wk_ref[...], wv_ref[...]], axis=1)
    out = jnp.dot(x, w, preferred_element_type=f32)
    width = wk_ref.shape[1]
    for b in range(width // hd):
        lanes = slice(b * hd, (b + 1) * hd)
        kv_ref[0, :, lanes] = normed(out[:, lanes], gain_ref[...])
    kv_ref[1] = out[:, width:].astype(bf16)


def add_total(s_ref, head, rows, total):
    here = (lane_id() & (hd // 2 - 1)) == head
    s_ref[rows, :] = jnp.where(here, s_ref[rows, :] + total, s_ref[rows, :])


def begin(s_ref, t_ref):
    @pl.when(pl.program_id(0) == 0)
    def _():
        s_ref[...] = jnp.zeros_like(s_ref) if t_ref is None else t_ref[...]


def gather(q_ref, a_ref, o_ref, s_ref, choices):
    step = pl.program_id(0)
    taken = None
    for condition, kv_refs, pairs, pieces in choices:
        taken = condition if taken is None else taken | condition

        def run(kv_refs=kv_refs, pairs=pairs, pieces=pieces):
            def sink(b, rows, lanes, out, total):
                o_ref[rows, lanes] = out if a_ref is None else a_ref[rows, lanes] + out
                add_total(s_ref, step * group + b, rows, total)

            attend_group(q_ref, kv_refs, pairs, pieces, sink)

        pl.when(condition)(run)

    @pl.when(jnp.logical_not(taken))
    def _():
        o_ref[...] = jnp.zeros_like(o_ref) if a_ref is None else a_ref[...]


def near_needed(ext, lens):
    needed = None
    for query_of in (itself, core_partner, y_partner):
        pairs, reach = reach_flags(query_of, itself, ext, lens)
        need = any_of(pairs) & reach
        needed = need if needed is None else needed | need
    return needed


def home_kernel(ext, lens, q_ref, x_ref, wk_ref, wv_ref, gain_ref, o_ref, s_ref, kv_ref, late_ref):
    step = pl.program_id(0)
    begin(s_ref, None)
    keys_values([x_ref], wk_ref, wv_ref, gain_ref, kv_ref)
    pairs, _ = reach_flags(itself, itself, ext, lens)
    gather(q_ref, None, o_ref, s_ref, [(any_of(pairs), [kv_ref], pairs, home_pieces())])

    @pl.when(step == 0)
    def _():
        late_ref[...] = x_ref[x_ref.shape[0] // 2 :, :]


def first_kernel(ext, lens, xu, xd, wk_ref, wv_ref, gain_ref, near_ref):
    @pl.when(near_needed(ext, lens))
    def _():
        keys_values([xu, xd], wk_ref, wv_ref, gain_ref, near_ref)


def y_kernel(ext, lens, q_ref, kv_ref, near_ref, o_ref, s_ref):
    begin(s_ref, None)
    pairs, reach = reach_flags(y_partner, itself, ext, lens)
    active = any_of(pairs)
    gather(
        q_ref,
        None,
        o_ref,
        s_ref,
        [
            (active & reach, [kv_ref, near_ref], pairs, home_pieces() + near_pieces([0])),
            (active & jnp.logical_not(reach), [kv_ref], pairs, home_pieces()),
        ],
    )


def second_kernel(
    ext, lens, xu, xd, wk_ref, wv_ref, gain_ref, q_ref, a_ref, t_ref, o_ref, near_ref, s_ref, part
):
    step = pl.program_id(0)
    begin(s_ref, t_ref)

    @pl.when(near_needed(ext, lens))
    def _():
        keys_values([xu, xd], wk_ref, wv_ref, gain_ref, near_ref)

    pairs, reach = reach_flags(y_partner, itself, ext, lens)
    gather(q_ref, a_ref, part, s_ref, [(any_of(pairs) & reach, [near_ref], pairs, near_pieces([1]))])
    width = part.shape[1]
    o_ref[:, pl.ds(pl.multiple_of(step * width, width), width)] = part[...].astype(bf16)

    @pl.when(step == pl.num_programs(0) - 1)
    def _():
        high = s_ref[...].astype(bf16)
        low = (s_ref[...] - high.astype(f32)).astype(bf16)
        o_ref[:, o_ref.shape[1] - hd :] = jnp.where(lane_id() < hd // 2, high, low)


def near_kernel(ext, lens, q_ref, a_ref, t_ref, first_ref, last_ref, o_ref, s_ref):
    begin(s_ref, t_ref)
    pairs, reach = reach_flags(itself, itself, ext, lens)
    keys = [first_ref, last_ref]
    gather(q_ref, a_ref, o_ref, s_ref, [(any_of(pairs) & reach, keys, pairs, near_pieces([0, 1]))])


def core_kernel(ext, lens, q_ref, a_ref, t_ref, home_ref, first_ref, last_ref, o_ref, s_ref, part):
    begin(s_ref, t_ref)
    pairs, reach = reach_flags(itself, core_partner, ext, lens)
    active = any_of(pairs)
    gather(
        q_ref,
        a_ref,
        part,
        s_ref,
        [
            (active & reach, [home_ref, first_ref, last_ref], pairs, home_pieces() + near_pieces([0, 1])),
            (active & jnp.logical_not(reach), [home_ref], pairs, home_pieces()),
        ],
    )
    o_ref[...] = part[...].astype(bf16)


def close_kernel(a_ref, t_ref, y_ref, w_ref, out_ref, mixed):
    width = a_ref.shape[1]
    back = y_ref[:, width:].astype(f32)
    for b in range(width // hd):
        lanes = slice(b * hd, (b + 1) * hd)
        low = hd // 2 + b
        total = t_ref[:, b : b + 1] + (back[:, b : b + 1] + back[:, low : low + 1])
        value = a_ref[:, lanes].astype(f32) + y_ref[:, lanes].astype(f32)
        mixed[:, lanes] = (value / total).astype(bf16)
    out_ref[...] = jnp.dot(mixed[...], w_ref[...], preferred_element_type=f32).astype(bf16)


def whole(shape):
    return pl.BlockSpec(shape, lambda g: (0,) * len(shape), pipeline_mode=pl.Buffered(1))


def by_group(rows):
    return pl.BlockSpec((rows, group * hd), lambda g: (0, g))


def call(kernel, steps, ins, outs, flops, scratch=(), after=None, vmem=vmem_other):
    run, specs, arrays = kernel, [spec for _, spec in ins], [array for array, _ in ins]
    if after is not None:
        place = len(ins)
        specs, arrays = specs + [pl.BlockSpec(memory_space=pl.ANY)], arrays + [after]

        def run(*refs):
            kernel(*refs[:place], *refs[place + 1 :])

    return pl.pallas_call(
        run,
        grid=(steps,),
        in_specs=specs,
        out_specs=[spec for spec, _, _ in outs],
        out_shape=[jax.ShapeDtypeStruct(shape, dtype) for _, shape, dtype in outs],
        scratch_shapes=list(scratch),
        compiler_params=pltpu.CompilerParams(vmem_limit_bytes=vmem),
        cost_estimate=pl.CostEstimate(flops=int(flops), bytes_accessed=1, transcendentals=0),
    )(*arrays)


def body(activations, qkv_weight, out_weight, query_gain, key_gain, clip_lengths, extents):
    frames, rows, cols, model = activations.shape
    half = rows * cols
    tile = frames * half
    inner = out_weight.shape[0]
    steps = inner // (group * hd)
    x = activations.reshape(tile, model)
    q_gain, k_gain = query_gain.reshape(1, hd), key_gain.reshape(1, hd)
    smem = pl.BlockSpec(memory_space=pltpu.SMEM)

    def swap(a, axis, first):
        route = [(i, i + 1) for i in range(first, lax.axis_size(axis) - 1, 2)]
        return lax.ppermute(a, axis, route + [(j, i) for i, j in route])

    def to_heights(a):
        return swap(a, "ha", 0), swap(a, "ha", 1)

    def to_core(a):
        return swap(a, "ta", 0)

    def to_y(a):
        return swap(a, "ta", 1)

    def w_of(part):
        return (qkv_weight, pl.BlockSpec((model, group * hd), lambda g: (0, part * steps + g)))

    unit = cost * 2.0 * tile * tile * inner
    mat = cost * 2.0 * tile * model * inner
    total_spec = whole((tile, hd))
    sums = [(by_group(tile), (tile, inner), f32), (total_spec, (tile, hd), f32)]
    kv_spec = pl.BlockSpec((2, tile, group * hd), lambda g: (0, 0, g))
    kv_out = (kv_spec, (2, tile, inner), bf16)
    flags = [(extents, smem), (clip_lengths, smem)]
    kv_weights = [w_of(1), w_of(2), (k_gain, whole((1, hd)))]

    up_first, down_first = to_heights(activations[0].reshape(half, model))
    (q,) = call(
        project_kernel,
        steps,
        [(x, whole((tile, model))), w_of(0), (q_gain, whole((1, hd)))],
        [(by_group(tile), (tile, inner), bf16)],
        mat,
        vmem=vmem_weights,
    )
    q_y = to_y(q)
    own, own_total, kv_home, late = call(
        home_kernel,
        steps,
        flags + [(q, by_group(tile)), (x, whole((tile, model)))] + kv_weights,
        sums + [kv_out, (whole((half, model)), (half, model), bf16)],
        unit + 2 * mat,
        vmem=vmem_weights,
    )
    up_last, down_last = to_heights(late)
    kv_core = to_core(kv_home)

    def partial(acc, total):
        return [(acc, by_group(tile)), (total, total_spec)]

    def neighbours(up, down):
        return [(up, whole((half, model))), (down, whole((half, model)))]

    (near_first,) = call(
        first_kernel,
        steps,
        flags + neighbours(up_first, down_first) + kv_weights,
        [kv_out],
        2 * mat,
        after=own_total,
        vmem=vmem_weights,
    )
    near_first_core = to_core(near_first)
    y, y_total = call(
        y_kernel,
        steps,
        flags + [(q_y, by_group(tile)), (kv_home, kv_spec), (near_first, kv_spec)],
        sums,
        2 * unit,
        vmem=vmem_weights,
    )
    wide = (tile, inner + hd)
    y_part, near_last = call(
        second_kernel,
        steps,
        flags + neighbours(up_last, down_last) + kv_weights + [(q_y, by_group(tile))] + partial(y, y_total),
        [(whole(wide), wide, bf16), kv_out],
        unit + 2 * mat,
        [pltpu.VMEM((tile, hd), f32), pltpu.VMEM((tile, group * hd), f32)],        vmem=vmem_weights,
    )
    y_back = to_y(y_part)
    near_last_core = to_core(near_last)

    own, own_total = call(
        near_kernel,
        steps,
        flags + [(q, by_group(tile))] + partial(own, own_total) + [(near_first, kv_spec), (near_last, kv_spec)],
        sums,
        2 * unit,
        vmem=vmem_weights,
    )
    own, own_total = call(
        core_kernel,
        steps,
        flags
        + [(q, by_group(tile))]
        + partial(own, own_total)
        + [(kv, kv_spec) for kv in (kv_core, near_first_core, near_last_core)],
        [(by_group(tile), (tile, inner), bf16), sums[1]],
        3 * unit,
        [pltpu.VMEM((tile, group * hd), f32)],
    )
    cut = tile // close_steps
    (result,) = call(
        close_kernel,
        close_steps,
        [(a, pl.BlockSpec((cut, a.shape[1]), lambda g: (g, 0))) for a in (own, own_total, y_back)]
        + [(out_weight, whole((inner, model)))],
        [(pl.BlockSpec((cut, model), lambda g: (g, 0)), (tile, model), bf16)],
        mat,
        [pltpu.VMEM((cut, inner), bf16)],
    )
    return result.reshape(frames, rows, cols, model)


def solution(mesh):
    placed = (P("ta", "ha", None, None), P(), P(), P(), P(), P(), P())
    return jax.shard_map(
        body, mesh=mesh, in_specs=placed, out_specs=P("ta", "ha", None, None), check_vma=False
    )
```

```python
import functools
import math

import jax
import jax.numpy as jnp
from jax import lax
from jax.experimental import pallas as pl
from jax.experimental.pallas import tpu as pltpu
from jax.sharding import PartitionSpec as P

norm_eps = 1e-06
f32 = jnp.float32
bf16 = jnp.bfloat16
hd = 128
group = 4
cost = 2.5
close_steps = 5
vmem_weights = 50 << 20
vmem_other = 20 << 20


def normed(features, gain):
    mean_sq = jnp.mean(features * features, axis=-1, keepdims=True)
    return (features * lax.rsqrt(mean_sq + norm_eps) * gain).astype(bf16)


def same_clip(first, second, lengths):
    end = 0
    same = None
    for c in range(lengths.shape[0] - 1):
        end = end + lengths[c]
        here = (first >= end) == (second >= end)
        same = here if same is None else same & here
    return same


def core_partner(t):
    return t + 1 - 2 * lax.rem(t, 2)


def y_partner(t):
    return t - 1 + 2 * lax.rem(t, 2)


def itself(t):
    return t


def reach_flags(query_of, key_of, extents, lengths):
    t, h = lax.axis_index("ta"), lax.axis_index("ha")
    count = lax.axis_size("ta")
    query, key = query_of(t), key_of(t)
    inside = (query >= 0) & (query < count) & (key >= 0) & (key < count)
    safe = jnp.clip(query, 0, count - 1)
    near = inside & (jnp.abs(query - key) <= extents[safe, h, 0])
    pairs = [[near & same_clip(2 * safe + i, 2 * key + j, lengths) for j in range(2)] for i in range(2)]
    return pairs, extents[safe, h, 1] >= 1


def any_of(pairs):
    return pairs[0][0] | pairs[0][1] | pairs[1][0] | pairs[1][1]


def home_pieces():
    return [(0, True), (1, True)]


def near_pieces(frames):
    h = lax.axis_index("ha")
    both = (h > 0) & (h < lax.axis_size("ha") - 1)
    return [(frame, side) for frame in frames for side in (True, both)]


def column_masks(pairs, half, pieces):
    where = lax.broadcasted_iota(jnp.int32, (1, half * len(pieces)), 1)
    masks = []
    for i in range(2):
        row = None
        for a, (frame, valid) in enumerate(pieces):
            on = (pairs[i][frame] & valid).astype(f32)
            part = jnp.where((where >= a * half) & (where < (a + 1) * half), on, 0.0)
            row = part if row is None else row + part
        masks.append(row)
    return masks


def attend(q, k, v, mask):
    scores = lax.dot_general(q, k, (((1,), (1,)), ((), ())), preferred_element_type=f32)
    weights = (jnp.exp2(scores * (math.log2(math.e) / math.sqrt(hd))) * mask).astype(bf16)
    wide = jnp.concatenate([v, jnp.ones_like(v)], axis=1)
    return jnp.dot(weights, wide, preferred_element_type=f32)


def attend_group(q_ref, kv_refs, pairs, pieces, sink):
    half = q_ref.shape[0] // 2
    masks = column_masks(pairs, half, pieces)
    for b in range(q_ref.shape[1] // hd):
        lanes = slice(b * hd, (b + 1) * hd)
        k = jnp.concatenate([ref[0, :, lanes] for ref in kv_refs], axis=0)
        v = jnp.concatenate([ref[1, :, lanes] for ref in kv_refs], axis=0)
        for i in range(2):
            rows = slice(i * half, (i + 1) * half)
            out = attend(q_ref[rows, lanes], k, v, masks[i])
            sink(b, rows, lanes, out[:, :hd], out[:, hd:])


def lane_id():
    return lax.broadcasted_iota(jnp.int32, (1, hd), 1)


def project_kernel(x_ref, w_ref, gain_ref, q_ref):
    out = jnp.dot(x_ref[...], w_ref[...], preferred_element_type=f32)
    for b in range(out.shape[1] // hd):
        lanes = slice(b * hd, (b + 1) * hd)
        q_ref[:, lanes] = normed(out[:, lanes], gain_ref[...])


def keys_values(x_refs, wk_ref, wv_ref, gain_ref, kv_ref):
    x = x_refs[0][...] if len(x_refs) == 1 else jnp.concatenate([ref[...] for ref in x_refs], axis=0)
    w = jnp.concatenate([wk_ref[...], wv_ref[...]], axis=1)
    out = jnp.dot(x, w, preferred_element_type=f32)
    width = wk_ref.shape[1]
    for b in range(width // hd):
        lanes = slice(b * hd, (b + 1) * hd)
        kv_ref[0, :, lanes] = normed(out[:, lanes], gain_ref[...])
    kv_ref[1] = out[:, width:].astype(bf16)


def add_total(s_ref, head, rows, total):
    here = (lane_id() & (hd // 2 - 1)) == head
    s_ref[rows, :] = jnp.where(here, s_ref[rows, :] + total, s_ref[rows, :])


def begin(s_ref, t_ref):
    @pl.when(pl.program_id(0) == 0)
    def _():
        s_ref[...] = jnp.zeros_like(s_ref) if t_ref is None else t_ref[...]


def gather(q_ref, a_ref, o_ref, s_ref, choices):
    step = pl.program_id(0)
    taken = None
    for condition, kv_refs, pairs, pieces in choices:
        taken = condition if taken is None else taken | condition

        def run(kv_refs=kv_refs, pairs=pairs, pieces=pieces):
            def sink(b, rows, lanes, out, total):
                o_ref[rows, lanes] = out if a_ref is None else a_ref[rows, lanes] + out
                add_total(s_ref, step * group + b, rows, total)

            attend_group(q_ref, kv_refs, pairs, pieces, sink)

        pl.when(condition)(run)

    @pl.when(jnp.logical_not(taken))
    def _():
        o_ref[...] = jnp.zeros_like(o_ref) if a_ref is None else a_ref[...].astype(o_ref.dtype)


def near_needed(ext, lens):
    needed = None
    for query_of in (itself, core_partner, y_partner):
        pairs, reach = reach_flags(query_of, itself, ext, lens)
        need = any_of(pairs) & reach
        needed = need if needed is None else needed | need
    return needed


def home_kernel(ext, lens, q_ref, x_ref, wk_ref, wv_ref, gain_ref, o_ref, s_ref, kv_ref, late_ref):
    step = pl.program_id(0)
    begin(s_ref, None)
    keys_values([x_ref], wk_ref, wv_ref, gain_ref, kv_ref)
    pairs, _ = reach_flags(itself, itself, ext, lens)
    gather(q_ref, None, o_ref, s_ref, [(any_of(pairs), [kv_ref], pairs, home_pieces())])

    @pl.when(step == 0)
    def _():
        late_ref[...] = x_ref[x_ref.shape[0] // 2 :, :]


def first_kernel(ext, lens, xu, xd, wk_ref, wv_ref, gain_ref, near_ref):
    @pl.when(near_needed(ext, lens))
    def _():
        keys_values([xu, xd], wk_ref, wv_ref, gain_ref, near_ref)


def y_kernel(ext, lens, q_ref, kv_ref, near_ref, o_ref, s_ref):
    begin(s_ref, None)
    pairs, reach = reach_flags(y_partner, itself, ext, lens)
    active = any_of(pairs)
    gather(
        q_ref,
        None,
        o_ref,
        s_ref,
        [
            (active & reach, [kv_ref, near_ref], pairs, home_pieces() + near_pieces([0])),
            (active & jnp.logical_not(reach), [kv_ref], pairs, home_pieces()),
        ],
    )


def second_kernel(
    ext, lens, xu, xd, wk_ref, wv_ref, gain_ref, q_ref, a_ref, t_ref, o_ref, near_ref, s_ref, part
):
    step = pl.program_id(0)
    begin(s_ref, t_ref)

    @pl.when(near_needed(ext, lens))
    def _():
        keys_values([xu, xd], wk_ref, wv_ref, gain_ref, near_ref)

    pairs, reach = reach_flags(y_partner, itself, ext, lens)
    gather(q_ref, a_ref, part, s_ref, [(any_of(pairs) & reach, [near_ref], pairs, near_pieces([1]))])
    width = part.shape[1]
    o_ref[:, pl.ds(pl.multiple_of(step * width, width), width)] = part[...].astype(bf16)

    @pl.when(step == pl.num_programs(0) - 1)
    def _():
        high = s_ref[...].astype(bf16)
        low = (s_ref[...] - high.astype(f32)).astype(bf16)
        o_ref[:, o_ref.shape[1] - hd :] = jnp.where(lane_id() < hd // 2, high, low)


def near_kernel(ext, lens, q_ref, a_ref, t_ref, first_ref, last_ref, o_ref, s_ref, part):
    begin(s_ref, t_ref)
    pairs, reach = reach_flags(itself, itself, ext, lens)
    keys = [first_ref, last_ref]
    gather(q_ref, a_ref, part, s_ref, [(any_of(pairs) & reach, keys, pairs, near_pieces([0, 1]))])
    o_ref[...] = part[...].astype(bf16)


def core_kernel(ext, lens, q_ref, a_ref, t_ref, home_ref, first_ref, last_ref, o_ref, s_ref, part):
    begin(s_ref, t_ref)
    pairs, reach = reach_flags(itself, core_partner, ext, lens)
    active = any_of(pairs)
    gather(
        q_ref,
        a_ref,
        part,
        s_ref,
        [
            (active & reach, [home_ref, first_ref, last_ref], pairs, home_pieces() + near_pieces([0, 1])),
            (active & jnp.logical_not(reach), [home_ref], pairs, home_pieces()),
        ],
    )
    o_ref[...] = part[...].astype(bf16)


def close_kernel(a_ref, t_ref, y_ref, w_ref, out_ref, mixed):
    width = a_ref.shape[1]
    back = y_ref[:, width:].astype(f32)
    for b in range(width // hd):
        lanes = slice(b * hd, (b + 1) * hd)
        low = hd // 2 + b
        total = t_ref[:, b : b + 1] + (back[:, b : b + 1] + back[:, low : low + 1])
        value = a_ref[:, lanes].astype(f32) + y_ref[:, lanes].astype(f32)
        mixed[:, lanes] = (value / total).astype(bf16)
    out_ref[...] = jnp.dot(mixed[...], w_ref[...], preferred_element_type=f32).astype(bf16)


def whole(shape):
    return pl.BlockSpec(shape, lambda g: (0,) * len(shape), pipeline_mode=pl.Buffered(1))


def by_group(rows):
    return pl.BlockSpec((rows, group * hd), lambda g: (0, g))


def call(kernel, steps, ins, outs, flops, scratch=(), after=None, vmem=vmem_other):
    run, specs, arrays = kernel, [spec for _, spec in ins], [array for array, _ in ins]
    if after is not None:
        place = len(ins)
        specs, arrays = specs + [pl.BlockSpec(memory_space=pl.ANY)], arrays + [after]

        def run(*refs):
            kernel(*refs[:place], *refs[place + 1 :])

    return pl.pallas_call(
        run,
        grid=(steps,),
        in_specs=specs,
        out_specs=[spec for spec, _, _ in outs],
        out_shape=[jax.ShapeDtypeStruct(shape, dtype) for _, shape, dtype in outs],
        scratch_shapes=list(scratch),
        compiler_params=pltpu.CompilerParams(vmem_limit_bytes=vmem),
        cost_estimate=pl.CostEstimate(flops=int(flops), bytes_accessed=1, transcendentals=0),
    )(*arrays)


def body(activations, qkv_weight, out_weight, query_gain, key_gain, clip_lengths, extents):
    frames, rows, cols, model = activations.shape
    half = rows * cols
    tile = frames * half
    inner = out_weight.shape[0]
    steps = inner // (group * hd)
    x = activations.reshape(tile, model)
    q_gain, k_gain = query_gain.reshape(1, hd), key_gain.reshape(1, hd)
    smem = pl.BlockSpec(memory_space=pltpu.SMEM)

    def swap(a, axis, first):
        route = [(i, i + 1) for i in range(first, lax.axis_size(axis) - 1, 2)]
        return lax.ppermute(a, axis, route + [(j, i) for i, j in route])

    def to_heights(a):
        return swap(a, "ha", 0), swap(a, "ha", 1)

    def to_core(a):
        return swap(a, "ta", 0)

    def to_y(a):
        return swap(a, "ta", 1)

    def w_of(part):
        return (qkv_weight, pl.BlockSpec((model, group * hd), lambda g: (0, part * steps + g)))

    unit = cost * 2.0 * tile * tile * inner
    mat = cost * 2.0 * tile * model * inner
    total_spec = whole((tile, hd))
    sums = [(by_group(tile), (tile, inner), f32), (total_spec, (tile, hd), f32)]
    kv_spec = pl.BlockSpec((2, tile, group * hd), lambda g: (0, 0, g))
    kv_out = (kv_spec, (2, tile, inner), bf16)
    flags = [(extents, smem), (clip_lengths, smem)]
    kv_weights = [w_of(1), w_of(2), (k_gain, whole((1, hd)))]

    up_first, down_first = to_heights(activations[0].reshape(half, model))
    (q,) = call(
        project_kernel,
        steps,
        [(x, whole((tile, model))), w_of(0), (q_gain, whole((1, hd)))],
        [(by_group(tile), (tile, inner), bf16)],
        mat,
        vmem=vmem_weights,
    )
    q_y = to_y(q)
    own, own_total, kv_home, late = call(
        home_kernel,
        steps,
        flags + [(q, by_group(tile)), (x, whole((tile, model)))] + kv_weights,
        sums + [kv_out, (whole((half, model)), (half, model), bf16)],
        unit + 2 * mat,
        vmem=vmem_weights,
    )
    up_last, down_last = to_heights(late)
    kv_core = to_core(kv_home)

    def partial(acc, total):
        return [(acc, by_group(tile)), (total, total_spec)]

    def neighbours(up, down):
        return [(up, whole((half, model))), (down, whole((half, model)))]

    (near_first,) = call(
        first_kernel,
        steps,
        flags + neighbours(up_first, down_first) + kv_weights,
        [kv_out],
        2 * mat,
        after=own_total,
        vmem=vmem_weights,
    )
    near_first_core = to_core(near_first)
    y, y_total = call(
        y_kernel,
        steps,
        flags + [(q_y, by_group(tile)), (kv_home, kv_spec), (near_first, kv_spec)],
        sums,
        2 * unit,
        vmem=vmem_weights,
    )
    wide = (tile, inner + hd)
    y_part, near_last = call(
        second_kernel,
        steps,
        flags + neighbours(up_last, down_last) + kv_weights + [(q_y, by_group(tile))] + partial(y, y_total),
        [(whole(wide), wide, bf16), kv_out],
        unit + 2 * mat,
        [pltpu.VMEM((tile, hd), f32), pltpu.VMEM((tile, group * hd), f32)],        vmem=vmem_weights,
    )
    y_back = to_y(y_part)
    near_last_core = to_core(near_last)

    own, own_total = call(
        near_kernel,
        steps,
        flags + [(q, by_group(tile))] + partial(own, own_total) + [(near_first, kv_spec), (near_last, kv_spec)],
        [(by_group(tile), (tile, inner), bf16), sums[1]],
        2 * unit,
        [pltpu.VMEM((tile, group * hd), f32)],
        vmem=vmem_weights,
    )
    own, own_total = call(
        core_kernel,
        steps,
        flags
        + [(q, by_group(tile))]
        + partial(own, own_total)
        + [(kv, kv_spec) for kv in (kv_core, near_first_core, near_last_core)],
        [(by_group(tile), (tile, inner), bf16), sums[1]],
        3 * unit,
        [pltpu.VMEM((tile, group * hd), f32)],
    )
    cut = tile // close_steps
    (result,) = call(
        close_kernel,
        close_steps,
        [(a, pl.BlockSpec((cut, a.shape[1]), lambda g: (g, 0))) for a in (own, own_total, y_back)]
        + [(out_weight, whole((inner, model)))],
        [(pl.BlockSpec((cut, model), lambda g: (g, 0)), (tile, model), bf16)],
        mat,
        [pltpu.VMEM((cut, inner), bf16)],
    )
    return result.reshape(frames, rows, cols, model)


def solution(mesh):
    placed = (P("ta", "ha", None, None), P(), P(), P(), P(), P(), P())
    return jax.shard_map(
        body, mesh=mesh, in_specs=placed, out_specs=P("ta", "ha", None, None), check_vma=False
    )
```
